256 devices in a mesh: tm: 16 (over x, y), band: 16 (over z, core).
Axes of the slice: x: 4, y: 4, z: 8, core: 2. Of those that a mesh axis runs over, the one named last changes fastest.
Arguments:
- features: bfloat16 [32, 128, 64, 256], P('tm', 'band'), may hold values from -31 to 31
- first_gain: float32 [256], replicated, may hold values from 0.1 to 1.9
- first_shift: float32 [256], replicated, may hold values from -3 to 3
- first_weight: bfloat16 [3, 3, 3, 256, 256], replicated, may hold values from -0.078125 to 0.078125
- second_gain: float32 [256], replicated, may hold values from 0.1 to 1.9
- second_shift: float32 [256], replicated, may hold values from -3 to 3
- second_weight: bfloat16 [3, 3, 3, 256, 256], replicated, may hold values from -0.078125 to 0.078125
Outputs:
- decoded: bfloat16 [32, 128, 64, 256], P('tm', 'band')
The draws below stay inside these ranges and needn't reach their ends.
All inputs are finite; a program needn't handle non-finite values.
Results may differ from the reference program's by a relative error of at most 0.012.
Values may be sent and summed in bfloat16 or wider, within the bound.
No kernel may reach another device: no remote copies, remote signals or barrier semaphores. Data moves between devices by JAX's collectives and lax.ppermute only.
A program may use at most 64 MiB of HBM per device.

```python
import math
import jax
import jax.numpy as jnp
from jax import lax

C = 256
GROUPS = 32
F_DEV = 2
ROW_DEV = 8
W = 64
FRAMES = 32
H = 128


def draw_features(key, part):
    key = jax.random.fold_in(key, 7)
    key_base, key_band, key_pair, key_chan, key_offset = jax.random.split(key, 5)
    frame_pos = jnp.arange(FRAMES, dtype=jnp.float32) / max(FRAMES - 1, 1)
    row_pos = jnp.arange(H, dtype=jnp.float32) / max(H - 1, 1)
    band_scale = jnp.exp(jax.random.uniform(key_band, (H // ROW_DEV,), jnp.float32, math.log(0.25), math.log(2.0)))
    pair_scale = jnp.exp(jax.random.uniform(key_pair, (FRAMES // F_DEV,), jnp.float32, math.log(0.25), math.log(2.0)))
    band_rows = jnp.repeat(band_scale, ROW_DEV)
    pair_frames = jnp.repeat(pair_scale, F_DEV)
    row_scale = pair_frames[:, None] * band_rows[None, :]
    trend = 0.5 + 0.6 * frame_pos[:, None] + 0.1 * row_pos[None, :]
    base = jnp.clip(jax.random.normal(key_base, (FRAMES, H, W, C), jnp.float32), -3.0, 3.0)
    chan_scale = jnp.exp(jax.random.uniform(key_chan, (C,), jnp.float32, math.log(0.5), math.log(1.6)))
    offset = jax.random.uniform(key_offset, (C,), jnp.float32, 0.5, 1.5)
    values = (trend * row_scale)[:, :, None, None] * (chan_scale * base + offset)
    return values.astype(jnp.bfloat16)


def noise(own_key, shape, deviation, bound, held_as=jnp.bfloat16):
    entries = jax.random.normal(own_key, shape, jnp.float32) * deviation
    return jnp.minimum(jnp.maximum(entries, -bound), bound).astype(held_as)


def setup_inputs(seed: int = 0) -> dict:
    key_of = jax.random.split(jax.random.key(seed), 8)
    features = draw_features(jax.random.fold_in(key_of[7], 71), 0)
    first_gain = jnp.clip(1.0 + 0.18 * jax.random.normal(key_of[1], (C,), jnp.float32), 0.1, 1.9)
    first_shift = noise(key_of[2], (C,), 0.5, 3.0, jnp.float32)
    first_weight = noise(key_of[3], (3, 3, 3, C, C), (27 * C) ** -0.5, 0.078125)
    second_gain = jnp.clip(1.0 + 0.18 * jax.random.normal(key_of[4], (C,), jnp.float32), 0.1, 1.9)
    second_shift = noise(key_of[5], (C,), 0.5, 3.0, jnp.float32)
    second_weight = noise(key_of[6], (3, 3, 3, C, C), (27 * C) ** -0.5, 0.078125)
    return dict(features=features, first_gain=first_gain, first_shift=first_shift, first_weight=first_weight, second_gain=second_gain, second_shift=second_shift, second_weight=second_weight)


EPSILON = 1e-06

def group_act(values, gain, shift):
    data = values.astype(jnp.float32)
    shaped = data.reshape(data.shape[:3] + (GROUPS, C // GROUPS))
    centre = lax.optimization_barrier(jnp.mean(shaped, axis=(0, 1, 2, 4)))
    centred = shaped - centre[:, None]
    variance = lax.optimization_barrier(jnp.mean(centred * centred, axis=(0, 1, 2, 4)))
    normed = (centred * lax.rsqrt(variance + EPSILON)[:, None]).reshape(data.shape) * gain + shift
    return jax.nn.silu(normed).astype(jnp.bfloat16)

def causal_conv(values, weight):
    padded = jnp.pad(values, ((2, 0), (1, 1), (1, 1), (0, 0)), mode='edge')
    result = lax.conv_general_dilated(padded[None], weight, (1, 1, 1), 'VALID', dimension_numbers=('NDHWC', 'DHWIO', 'NDHWC'), preferred_element_type=jnp.float32)
    return result[0]

def reference(features, first_gain, first_shift, first_weight, second_gain, second_shift, second_weight):
    first_act = group_act(features, first_gain, first_shift)
    hidden = causal_conv(first_act, first_weight).astype(jnp.bfloat16)
    second_act = group_act(hidden, second_gain, second_shift)
    return (features.astype(jnp.float32) + causal_conv(second_act, second_weight)).astype(jnp.bfloat16)
```

```python
import functools

import jax
import jax.numpy as jnp
from jax import lax
from jax.experimental import pallas as pl
from jax.experimental.pallas import tpu as pltpu
from jax.sharding import PartitionSpec as P

GROUPS = 32
EPSILON = 1e-06
AXES = ("tm", "band")
LANES = 128
VMEM_LIMIT = 32 * 1024 * 1024
HIGHEST = lax.Precision.HIGHEST


def shifted(value, axis, by):
    count = lax.axis_size(axis)
    pairs = [(i, i + by) for i in range(count) if 0 <= i + by < count]
    return lax.ppermute(value, axis, pairs)


def shifted_both(value, tm_by, band_by):
    tm, band = lax.axis_size("tm"), lax.axis_size("band")
    pairs = [
        (t * band + b, (t + tm_by) * band + b + band_by)
        for t in range(tm)
        for b in range(band)
        if 0 <= t + tm_by < tm and 0 <= b + band_by < band
    ]
    return lax.ppermute(value, AXES, pairs)


def indicator(rows, cols, fn):
    r = lax.broadcasted_iota(jnp.int32, (rows, cols), 0)
    c = lax.broadcasted_iota(jnp.int32, (rows, cols), 1)
    return jnp.where(fn(r, c), 1.0, 0.0).astype(jnp.float32)


def exact_dot(a, b):
    return jnp.dot(a, b, precision=HIGHEST, preferred_element_type=jnp.float32)


def folded(block):
    cols, channels = block.shape
    return jnp.sum(block.reshape(cols // 8, 8, channels), axis=0)


def local_moments(rows, channels):
    size = channels // GROUPS
    total = folded(rows[0]().astype(jnp.float32))
    for row in rows[1:]:
        total = total + folded(row().astype(jnp.float32))
    positions = len(rows) * rows[0]().shape[0]
    channel_mean = jnp.sum(total, axis=0, keepdims=True) * (1.0 / positions)
    channel_mean = jnp.broadcast_to(channel_mean, (8, channels))
    same = indicator(channels, channels, lambda r, c: r // size == c // size)
    group_mean = exact_dot(channel_mean, same) * (1.0 / size)
    centre = group_mean[:1]
    spread = None
    for row in rows:
        off = row().astype(jnp.float32) - centre
        part = folded(off * off)
        spread = part if spread is None else spread + part
    first = indicator(channels, LANES, lambda r, c: r // size == c)
    second = indicator(channels, LANES, lambda r, c: r // size + GROUPS == c)
    spread = jnp.broadcast_to(jnp.sum(spread, axis=0, keepdims=True), (8, channels))
    line = exact_dot(channel_mean, first) * (1.0 / size) + exact_dot(spread, second)
    return line[:1]


def merged_moments(lines, members, channels):
    size = channels // GROUPS
    devices = lines.shape[0]
    mean = jnp.sum(lines, axis=0, keepdims=True) * (1.0 / devices)
    off = lines - mean
    between = jnp.sum(off * off, axis=0, keepdims=True) * (1.0 / devices)
    within = mean * (1.0 / members)
    pick_first = indicator(LANES, channels, lambda r, c: c // size == r)
    pick_second = indicator(LANES, channels, lambda r, c: c // size + GROUPS == r)
    wide = lambda line, pick: exact_dot(jnp.broadcast_to(line, (8, LANES)), pick)[:1]
    centre = wide(mean, pick_first)
    variance = wide(within, pick_second) + wide(between, pick_first)
    return centre, lax.rsqrt(variance + EPSILON)


def activated(x, centre, scale, offset):
    half = (x.astype(jnp.float32) - centre) * scale + offset
    return (half + half * jnp.tanh(half)).astype(jnp.bfloat16)


def load_weight(weight_ref, held_ref, sems):
    channels, outputs = weight_ref.shape[2:]
    copies = []
    for ij in range(9):
        for k in range(3):
            copies.append(
                pltpu.make_async_copy(
                    weight_ref.at[ij, k],
                    held_ref.at[pl.ds(ij * channels, channels), pl.ds(k * outputs, outputs)],
                    sems.at[ij * 3 + k],
                )
            )
    return copies


def convolved(act_ref, held_ref, frame, row_count):
    cols, channels = act_ref.shape[2:]
    outputs = held_ref.shape[1] // 3
    window = jnp.concatenate(
        [
            act_ref[frame + i, j : j + row_count].reshape(row_count * cols, channels)
            for i in range(3)
            for j in range(3)
        ],
        axis=-1,
    )
    taps = jnp.dot(window, held_ref[...], preferred_element_type=jnp.float32)
    taps = taps.reshape(row_count, cols, 3 * outputs)
    column = lax.broadcasted_iota(jnp.int32, (row_count, cols, outputs), 1)
    left = taps[..., :outputs]
    right = taps[..., 2 * outputs :]
    left = jnp.where(column == 0, left, pltpu.roll(left, 1, 1))
    right = jnp.where(column == cols - 1, right, pltpu.roll(right, cols - 1, 1))
    return left + taps[..., outputs : 2 * outputs] + right


def stats_kernel(x_ref, line_ref):
    frames, rows, _, channels = x_ref.shape
    reads = [functools.partial(lambda f, r: x_ref[f, r], f, r) for f in range(frames) for r in range(rows)]
    line_ref[...] = jnp.broadcast_to(local_moments(reads, channels), line_ref.shape)


def first_kernel(members, x_ref, prev_ref, up_ref, down_ref, prev_up_ref, prev_down_ref, lines_ref, gain_ref, shift_ref,
                 weight_ref, hidden_ref, line_ref, act_ref, held_ref, sems):
    copies = load_weight(weight_ref, held_ref, sems)
    for copy in copies:
        copy.start()
    frames, rows, cols, channels = x_ref.shape
    leading = lax.axis_index("tm") == 0
    top = lax.axis_index("band") == 0
    bottom = lax.axis_index("band") == lax.axis_size("band") - 1
    centre, inverse = merged_moments(lines_ref[...], members, channels)
    scale = 0.5 * inverse * gain_ref[...]
    offset = 0.5 * shift_ref[...]

    def own(f, r):
        if r == 0:
            return up_ref[f, 0]
        if r == 1:
            return jnp.where(top, x_ref[f, 0], up_ref[f, 1])
        if r == rows + 2:
            return jnp.where(bottom, x_ref[f, rows - 1], down_ref[f, 0])
        if r == rows + 3:
            return down_ref[f, 1]
        return x_ref[f, r - 2]

    def before(f, r):
        if r == 0:
            return prev_up_ref[f, 0]
        if r == 1:
            return jnp.where(top, prev_ref[f, 0], prev_up_ref[f, 1])
        if r == rows + 2:
            return jnp.where(bottom, prev_ref[f, rows - 1], prev_down_ref[f, 0])
        if r == rows + 3:
            return prev_down_ref[f, 1]
        return prev_ref[f, r - 2]

    for f in range(2 + frames):
        for r in range(rows + 4):
            x = jnp.where(leading, own(0, r), before(f, r)) if f < 2 else own(f - 2, r)
            act_ref[f, r] = activated(x, centre, scale, offset)
    for copy in copies:
        copy.wait()
    for f in range(frames):
        hidden_ref[f] = convolved(act_ref, held_ref, f, rows + 2).astype(jnp.bfloat16)
    reads = [
        functools.partial(lambda f, r: hidden_ref[f, r + 1], f, r) for f in range(frames) for r in range(rows)
    ]
    line_ref[...] = jnp.broadcast_to(local_moments(reads, channels), line_ref.shape)


def second_kernel(members, hidden_ref, prev_ref, lines_ref, gain_ref, shift_ref, x_ref, weight_ref, out_ref, act_ref,
                  held_ref, sems):
    copies = load_weight(weight_ref, held_ref, sems)
    for copy in copies:
        copy.start()
    frames, rows, cols, channels = x_ref.shape
    leading = lax.axis_index("tm") == 0
    top = lax.axis_index("band") == 0
    bottom = lax.axis_index("band") == lax.axis_size("band") - 1
    centre, inverse = merged_moments(lines_ref[...], members, channels)
    scale = 0.5 * inverse * gain_ref[...]
    offset = 0.5 * shift_ref[...]

    def row_of(ref, f, r):
        if r == 0:
            return jnp.where(top, ref[f, 1], ref[f, 0])
        if r == rows + 1:
            return jnp.where(bottom, ref[f, rows], ref[f, rows + 1])
        return ref[f, r]

    for f in range(2 + frames):
        for r in range(rows + 2):
            if f < 2:
                x = jnp.where(leading, row_of(hidden_ref, 0, r), row_of(prev_ref, f, r))
            else:
                x = row_of(hidden_ref, f - 2, r)
            act_ref[f, r] = activated(x, centre, scale, offset)
    for copy in copies:
        copy.wait()
    for f in range(frames):
        out_ref[f] = (x_ref[f].astype(jnp.float32) + convolved(act_ref, held_ref, f, rows)).astype(jnp.bfloat16)


def local(
    features, first_gain, first_shift, first_weight, second_gain, second_shift, second_weight
):
    frames, rows, cols, channels = features.shape
    outputs = first_weight.shape[-1]
    devices = lax.axis_size("tm") * lax.axis_size("band")
    members = frames * rows * cols * (channels // GROUPS)
    vmem = pl.BlockSpec(memory_space=pltpu.VMEM)
    anywhere = pl.BlockSpec(memory_space=pl.ANY)
    params = pltpu.CompilerParams(vmem_limit_bytes=VMEM_LIMIT)
    line = jax.ShapeDtypeStruct((devices, LANES), jnp.float32)
    row = lambda vector: vector.reshape(1, channels)
    taps = lambda weight: weight.reshape(9, 3, channels, outputs)
    scratch = lambda halo_rows: [
        pltpu.VMEM((frames + 2, rows + halo_rows, cols, channels), jnp.bfloat16),
        pltpu.VMEM((9 * channels, 3 * outputs), jnp.bfloat16),
        pltpu.SemaphoreType.DMA((27,)),
    ]

    bottom_rows = features[:, rows - 2 :]
    top_rows = features[:, :2]
    prev = shifted(features, "tm", 1)
    up = shifted(bottom_rows, "band", 1)
    down = shifted(top_rows, "band", -1)
    prev_up = shifted_both(bottom_rows, 1, 1)
    prev_down = shifted_both(top_rows, 1, -1)
    lines = pl.pallas_call(
        stats_kernel, out_shape=line, in_specs=[vmem], out_specs=vmem, compiler_params=params, name="moments"
    )(features)
    lines = lax.all_to_all(lines, AXES, 0, 0, tiled=True)

    hidden, lines = pl.pallas_call(
        functools.partial(first_kernel, members),
        out_shape=[jax.ShapeDtypeStruct((frames, rows + 2, cols, outputs), jnp.bfloat16), line],
        in_specs=[vmem] * 9 + [anywhere],
        out_specs=[vmem, vmem],
        scratch_shapes=scratch(4),
        compiler_params=params,
        name="first_conv",
    )(features, prev, up, down, prev_up, prev_down, lines, row(first_gain), row(first_shift), taps(first_weight))

    prev = shifted(hidden, "tm", 1)
    lines = lax.all_to_all(lines, AXES, 0, 0, tiled=True)

    return pl.pallas_call(
        functools.partial(second_kernel, members),
        out_shape=jax.ShapeDtypeStruct(features.shape, jnp.bfloat16),
        in_specs=[vmem] * 6 + [anywhere],
        out_specs=vmem,
        scratch_shapes=scratch(2),
        compiler_params=params,
        name="second_conv",
    )(hidden, prev, lines, row(second_gain), row(second_shift), features, taps(second_weight))


def solution(mesh):
    in_specs = (P("tm", "band", None, None), P(), P(), P(), P(), P(), P())
    out_specs = P("tm", "band", None, None)
    return jax.shard_map(local, mesh=mesh, in_specs=in_specs, out_specs=out_specs, check_vma=False)
```

```python
import functools

import jax
import jax.numpy as jnp
from jax import lax
from jax.experimental import pallas as pl
from jax.experimental.pallas import tpu as pltpu
from jax.sharding import PartitionSpec as P

GROUPS = 32
EPSILON = 1e-06
LANES = 128
VMEM_LIMIT = 32 * 1024 * 1024
HIGHEST = lax.Precision.HIGHEST


def next_frames(value):
    count = lax.axis_size("tm")
    return lax.ppermute(value, "tm", [(i, i + 1) for i in range(count - 1)])


def swapped(value, axis, first):
    count = lax.axis_size(axis)
    pairs = []
    for i in range(first, count - 1, 2):
        pairs += [(i, i + 1), (i + 1, i)]
    return lax.ppermute(value, axis, pairs)


def indicator(rows, cols, fn):
    r = lax.broadcasted_iota(jnp.int32, (rows, cols), 0)
    c = lax.broadcasted_iota(jnp.int32, (rows, cols), 1)
    return jnp.where(fn(r, c), 1.0, 0.0).astype(jnp.float32)


def exact_dot(a, b):
    return jnp.dot(a, b, precision=HIGHEST, preferred_element_type=jnp.float32)


def folded(block):
    cols, channels = block.shape
    return jnp.sum(block.reshape(cols // 8, 8, channels), axis=0)


def local_moments(rows, channels):
    size = channels // GROUPS
    total = folded(rows[0]().astype(jnp.float32))
    for row in rows[1:]:
        total = total + folded(row().astype(jnp.float32))
    positions = len(rows) * rows[0]().shape[0]
    channel_mean = jnp.sum(total, axis=0, keepdims=True) * (1.0 / positions)
    channel_mean = jnp.broadcast_to(channel_mean, (8, channels))
    same = indicator(channels, channels, lambda r, c: r // size == c // size)
    group_mean = exact_dot(channel_mean, same) * (1.0 / size)
    centre = group_mean[:1]
    spread = None
    for row in rows:
        off = row().astype(jnp.float32) - centre
        part = folded(off * off)
        spread = part if spread is None else spread + part
    first = indicator(channels, LANES, lambda r, c: r // size == c)
    second = indicator(channels, LANES, lambda r, c: r // size + GROUPS == c)
    spread = jnp.broadcast_to(jnp.sum(spread, axis=0, keepdims=True), (8, channels))
    line = exact_dot(channel_mean, first) * (1.0 / size) + exact_dot(spread, second)
    return line[:1]


def merged_lines(lines, members):
    count = lines.shape[0]
    total = jnp.sum(lines, axis=0, keepdims=True)
    mean = total * (1.0 / count)
    off = lines - mean
    between = jnp.sum(off * off, axis=0, keepdims=True) * members
    lane = lax.broadcasted_iota(jnp.int32, (1, LANES), 1)
    between = jnp.broadcast_to(between, (8, LANES))
    between = pltpu.roll(between, GROUPS, 1)[:1]
    return jnp.where(lane < GROUPS, mean, jnp.where(lane < 2 * GROUPS, total + between, 0.0))


def channel_moments(line, members, channels):
    size = channels // GROUPS
    pick_first = indicator(LANES, channels, lambda r, c: c // size == r)
    pick_second = indicator(LANES, channels, lambda r, c: c // size + GROUPS == r)
    line = jnp.broadcast_to(line, (8, LANES))
    centre = exact_dot(line, pick_first)[:1]
    variance = exact_dot(line, pick_second)[:1] * (1.0 / members)
    return centre, lax.rsqrt(variance + EPSILON)


def activated(x, centre, scale, offset):
    half = (x.astype(jnp.float32) - centre) * scale + offset
    return (half + half * jnp.tanh(half)).astype(jnp.bfloat16)


def convolved(act_ref, weight_ref, frame, row_count):
    cols, channels = act_ref.shape[2:]
    outputs = weight_ref.shape[-1]
    window = jnp.concatenate(
        [
            act_ref[frame + i, j : j + row_count].reshape(row_count * cols, channels)
            for i in range(3)
            for j in range(3)
        ],
        axis=-1,
    )
    left, middle, right = (
        jnp.dot(
            window,
            weight_ref[:, k].reshape(9 * channels, outputs),
            preferred_element_type=jnp.float32,
        ).reshape(row_count, cols, outputs)
        for k in range(3)
    )
    column = lax.broadcasted_iota(jnp.int32, (row_count, cols, outputs), 1)
    left = jnp.where(column == 0, left, pltpu.roll(left, 1, 1))
    right = jnp.where(column == cols - 1, right, pltpu.roll(right, cols - 1, 1))
    return left + middle + right


def places(rows):
    even = lax.rem(lax.axis_index("band"), 2) == 0
    pair_at, cross_at = jnp.where(even, rows + 2, 0), jnp.where(even, 0, rows + 2)
    pair_from, cross_from = jnp.where(even, rows - 2, 0), jnp.where(even, 0, rows - 2)
    return pair_at, cross_at, pair_from, cross_from


def stats_kernel(x_ref, *refs):
    vectors, (line_ref, kept_ref, params_ref, sems) = refs[:4], refs[4:]
    frames, rows, _, channels = x_ref.shape
    copies = [pltpu.make_async_copy(x_ref.at[f], kept_ref.at[f], sems.at[f]) for f in range(frames)]
    copies += [
        pltpu.make_async_copy(vector, params_ref.at[pl.ds(i, 1)], sems.at[frames + i])
        for i, vector in enumerate(vectors)
    ]
    for copy in copies:
        copy.start()
    for copy in copies:
        copy.wait()
    reads = [functools.partial(lambda f, r: kept_ref[f, r], f, r) for f in range(frames) for r in range(rows)]
    line_ref[...] = jnp.broadcast_to(local_moments(reads, channels), line_ref.shape)


def edges_kernel(members, lines_ref, x_ref, prev_ref, line_ref, pair_ref, cross_ref):
    rows = x_ref.shape[1]
    _, _, pair_from, cross_from = places(rows)
    for out_ref, at in ((pair_ref, pair_from), (cross_ref, cross_from)):
        out_ref[0:2] = prev_ref[:, pl.ds(at, 2)]
        out_ref[2:4] = x_ref[:, pl.ds(at, 2)]
    line_ref[...] = jnp.broadcast_to(merged_lines(lines_ref[...], members), line_ref.shape)


def merge_kernel(members, lines_ref, line_ref):
    line_ref[...] = jnp.broadcast_to(merged_lines(lines_ref[...], members), line_ref.shape)


def scaling(lines_ref, params_ref, norm, members):
    channels = params_ref.shape[1]
    devices = lax.axis_size("tm") * lax.axis_size("band")
    line = merged_lines(lines_ref[...], members * lax.axis_size("band"))
    centre, inverse = channel_moments(line, members * devices, channels)
    gain, shift = params_ref[2 * norm : 2 * norm + 1], params_ref[2 * norm + 1 : 2 * norm + 2]
    return centre, 0.5 * inverse * gain, 0.5 * shift


def at_ends():
    band = lax.axis_index("band")
    return lax.axis_index("tm") == 0, band == 0, band == lax.axis_size("band") - 1


def first_kernel(members, x_ref, prev_ref, pair_ref, cross_ref, lines_ref, params_ref, weight_ref,
                 hidden_ref, line_ref, act_ref, held_ref, weight_sems):
    frames, rows, cols, channels = x_ref.shape
    weights = [pltpu.make_async_copy(weight_ref.at[t], held_ref.at[t], weight_sems.at[t]) for t in range(9)]
    for copy in weights:
        copy.start()
    leading, top, bottom = at_ends()
    even = lax.rem(lax.axis_index("band"), 2) == 0
    norm = scaling(lines_ref, params_ref, 0, members)

    def row_of(f, r):
        inner = prev_ref if f < 2 else x_ref
        if 2 <= r < rows + 2:
            return inner[f % 2, r - 2]
        if r < 2:
            outer = jnp.where(even, cross_ref[f, r], pair_ref[f, r])
            return jnp.where(top, inner[f % 2, 0], outer) if r == 1 else outer
        outer = jnp.where(even, pair_ref[f, r - rows - 2], cross_ref[f, r - rows - 2])
        return jnp.where(bottom, inner[f % 2, rows - 1], outer) if r == rows + 2 else outer

    def activate(f):
        for r in range(rows + 4):
            x = jnp.where(leading, row_of(2, r), row_of(f, r)) if f < 2 else row_of(f, r)
            act_ref[f, r] = activated(x, *norm)

    for f in range(2 + frames):
        activate(f)
    for copy in weights:
        copy.wait()
    for f in range(frames):
        hidden_ref[f] = convolved(act_ref, held_ref, f, rows + 2).astype(jnp.bfloat16)
    reads = [functools.partial(lambda f, r: hidden_ref[f, r + 1], f, r) for f in range(frames) for r in range(rows)]
    line_ref[...] = jnp.broadcast_to(local_moments(reads, channels), line_ref.shape)


def second_kernel(members, hidden_ref, prev_ref, lines_ref, params_ref, x_ref, weight_ref, out_ref,
                  act_ref, made_ref, out_sems):
    frames, rows, cols, channels = x_ref.shape
    leading, top, bottom = at_ends()
    norm = scaling(lines_ref, params_ref, 1, members)

    def row_of(f, r):
        ref = prev_ref if f < 2 else hidden_ref
        if r == 0:
            return jnp.where(top, ref[f % 2, 1], ref[f % 2, 0])
        if r == rows + 1:
            return jnp.where(bottom, ref[f % 2, rows], ref[f % 2, rows + 1])
        return ref[f % 2, r]

    def activate(f):
        for r in range(rows + 2):
            x = jnp.where(leading, row_of(2, r), row_of(f, r)) if f < 2 else row_of(f, r)
            act_ref[f, r] = activated(x, *norm)

    for f in range(2 + frames):
        activate(f)
    outs = []
    for f in range(frames):
        made_ref[f] = (x_ref[f].astype(jnp.float32) + convolved(act_ref, weight_ref, f, rows)).astype(jnp.bfloat16)
        outs.append(pltpu.make_async_copy(made_ref.at[f], out_ref.at[f], out_sems.at[f]))
        outs[-1].start()
    for copy in outs:
        copy.wait()


def local(
    features, first_gain, first_shift, first_weight, second_gain, second_shift, second_weight
):
    frames, rows, cols, channels = features.shape
    outputs = first_weight.shape[-1]
    tm, band = lax.axis_size("tm"), lax.axis_size("band")
    members = frames * rows * cols * (channels // GROUPS)
    vmem = pl.BlockSpec(memory_space=pltpu.VMEM)
    hbm = pl.BlockSpec(memory_space=pltpu.HBM)
    params = pltpu.CompilerParams(vmem_limit_bytes=VMEM_LIMIT)
    small = pltpu.CompilerParams(vmem_limit_bytes=4 * 1024 * 1024)
    line = lambda count: jax.ShapeDtypeStruct((count, LANES), jnp.float32)
    block = lambda f, r: jax.ShapeDtypeStruct((f, r, cols, channels), jnp.bfloat16)
    held = lambda f, r: pltpu.VMEM((f, r, cols, channels), jnp.bfloat16)
    dmas = lambda count: pltpu.SemaphoreType.DMA((count,))
    taps = lambda weight: weight.reshape(9, 3, channels, outputs)
    stay = lambda value: pltpu.with_memory_space_constraint(value, pltpu.HBM)
    spread_over = lambda lines, axis: lax.all_to_all(lines, axis, 0, 0, tiled=True)
    vectors = [v.reshape(1, channels) for v in (first_gain, first_shift, second_gain, second_shift)]

    prev = next_frames(features)
    lines, kept, vectors = pl.pallas_call(
        stats_kernel,
        out_shape=[line(band), block(frames, rows), jax.ShapeDtypeStruct((8, channels), jnp.float32)],
        in_specs=[hbm] * 5,
        out_specs=[vmem] * 3,
        scratch_shapes=[dmas(frames + 4)],
        compiler_params=small,
        name="moments",
    )(stay(features), *[stay(v) for v in vectors])
    lines = spread_over(lines, "band")
    lines, pair, cross = pl.pallas_call(
        functools.partial(edges_kernel, members),
        out_shape=[line(tm), block(frames + 2, 2), block(frames + 2, 2)],
        in_specs=[vmem] * 3,
        out_specs=[vmem] * 3,
        compiler_params=small,
        name="edges",
    )(lines, kept, prev)
    pair = swapped(pair, "band", 0)
    cross = swapped(cross, "band", 1)
    lines = spread_over(lines, "tm")

    hidden, lines = pl.pallas_call(
        functools.partial(first_kernel, members),
        out_shape=[block(frames, rows + 2), line(band)],
        in_specs=[vmem] * 6 + [hbm],
        out_specs=[vmem, vmem],
        scratch_shapes=[held(frames + 2, rows + 4), pltpu.VMEM((9, 3, channels, outputs), jnp.bfloat16), dmas(9)],
        compiler_params=params,
        name="first_conv",
    )(kept, prev, pair, cross, lines, vectors, stay(taps(first_weight)))

    prev = next_frames(hidden)
    lines = spread_over(lines, "band")
    lines = pl.pallas_call(
        functools.partial(merge_kernel, members),
        out_shape=line(tm),
        in_specs=[vmem],
        out_specs=vmem,
        compiler_params=small,
        name="merge",
    )(lines)
    lines = spread_over(lines, "tm")

    return pl.pallas_call(
        functools.partial(second_kernel, members),
        out_shape=block(frames, rows),
        in_specs=[vmem] * 6,
        out_specs=hbm,
        scratch_shapes=[held(frames + 2, rows + 2), held(frames, rows), dmas(frames)],
        compiler_params=params,
        name="second_conv",
    )(hidden, prev, lines, vectors, kept, taps(second_weight))


def solution(mesh):
    in_specs = (P("tm", "band", None, None), P(), P(), P(), P(), P(), P())
    out_specs = P("tm", "band", None, None)
    return jax.shard_map(local, mesh=mesh, in_specs=in_specs, out_specs=out_specs, check_vma=False)
```

```python
import functools

import jax
import jax.numpy as jnp
from jax import lax
from jax.experimental import pallas as pl
from jax.experimental.pallas import tpu as pltpu
from jax.sharding import PartitionSpec as P

GROUPS = 32
EPSILON = 1e-06
LANES = 128
VMEM_LIMIT = 32 * 1024 * 1024
HIGHEST = lax.Precision.HIGHEST


def next_frames(value):
    count = lax.axis_size("tm")
    return lax.ppermute(value, "tm", [(i, i + 1) for i in range(count - 1)])


def swapped(value, axis, first):
    count = lax.axis_size(axis)
    pairs = []
    for i in range(first, count - 1, 2):
        pairs += [(i, i + 1), (i + 1, i)]
    return lax.ppermute(value, axis, pairs)


def indicator(rows, cols, fn):
    r = lax.broadcasted_iota(jnp.int32, (rows, cols), 0)
    c = lax.broadcasted_iota(jnp.int32, (rows, cols), 1)
    return jnp.where(fn(r, c), 1.0, 0.0).astype(jnp.float32)


def exact_dot(a, b):
    return jnp.dot(a, b, precision=HIGHEST, preferred_element_type=jnp.float32)


def folded(block):
    cols, channels = block.shape
    return jnp.sum(block.reshape(cols // 8, 8, channels), axis=0)


def local_moments(rows, channels):
    size = channels // GROUPS
    total = folded(rows[0]().astype(jnp.float32))
    for row in rows[1:]:
        total = total + folded(row().astype(jnp.float32))
    positions = len(rows) * rows[0]().shape[0]
    channel_mean = jnp.sum(total, axis=0, keepdims=True) * (1.0 / positions)
    channel_mean = jnp.broadcast_to(channel_mean, (8, channels))
    same = indicator(channels, channels, lambda r, c: r // size == c // size)
    group_mean = exact_dot(channel_mean, same) * (1.0 / size)
    centre = group_mean[:1]
    spread = None
    for row in rows:
        off = row().astype(jnp.float32) - centre
        part = folded(off * off)
        spread = part if spread is None else spread + part
    first = indicator(channels, LANES, lambda r, c: r // size == c)
    second = indicator(channels, LANES, lambda r, c: r // size + GROUPS == c)
    spread = jnp.broadcast_to(jnp.sum(spread, axis=0, keepdims=True), (8, channels))
    line = exact_dot(channel_mean, first) * (1.0 / size) + exact_dot(spread, second)
    return line[:1]


def merged_lines(lines, members):
    count = lines.shape[0]
    total = jnp.sum(lines, axis=0, keepdims=True)
    mean = total * (1.0 / count)
    off = lines - mean
    between = jnp.sum(off * off, axis=0, keepdims=True) * members
    lane = lax.broadcasted_iota(jnp.int32, (1, LANES), 1)
    between = jnp.broadcast_to(between, (8, LANES))
    between = pltpu.roll(between, GROUPS, 1)[:1]
    return jnp.where(lane < GROUPS, mean, jnp.where(lane < 2 * GROUPS, total + between, 0.0))


def channel_moments(line, members, channels):
    size = channels // GROUPS
    pick_first = indicator(LANES, channels, lambda r, c: c // size == r)
    pick_second = indicator(LANES, channels, lambda r, c: c // size + GROUPS == r)
    line = jnp.broadcast_to(line, (8, LANES))
    centre = exact_dot(line, pick_first)[:1]
    variance = exact_dot(line, pick_second)[:1] * (1.0 / members)
    return centre, lax.rsqrt(variance + EPSILON)


def activated(x, centre, scale, offset):
    half = (x.astype(jnp.float32) - centre) * scale + offset
    return (half + half * jnp.tanh(half)).astype(jnp.bfloat16)


def convolved(act_ref, weight_of, frame, first_row, row_count):
    cols, channels = act_ref.shape[2:]
    window = jnp.concatenate(
        [
            act_ref[frame + i, first_row + j : first_row + j + row_count].reshape(row_count * cols, channels)
            for i in range(3)
            for j in range(3)
        ],
        axis=-1,
    )
    left, middle, right = (
        jnp.dot(window, weight_of(k), preferred_element_type=jnp.float32).reshape(row_count, cols, -1)
        for k in range(3)
    )
    column = lax.broadcasted_iota(jnp.int32, left.shape, 1)
    left = jnp.where(column == 0, left, pltpu.roll(left, 1, 1))
    right = jnp.where(column == cols - 1, right, pltpu.roll(right, cols - 1, 1))
    return left + middle + right


def places(rows):
    even = lax.rem(lax.axis_index("band"), 2) == 0
    pair_at, cross_at = jnp.where(even, rows + 2, 0), jnp.where(even, 0, rows + 2)
    pair_from, cross_from = jnp.where(even, rows - 2, 0), jnp.where(even, 0, rows - 2)
    return pair_at, cross_at, pair_from, cross_from


def stats_kernel(x_ref, *refs):
    vectors, (line_ref, kept_ref, params_ref, sems) = refs[:4], refs[4:]
    frames, rows, _, channels = x_ref.shape
    copies = [pltpu.make_async_copy(x_ref.at[f], kept_ref.at[f], sems.at[f]) for f in range(frames)]
    copies += [
        pltpu.make_async_copy(vector, params_ref.at[pl.ds(i, 1)], sems.at[frames + i])
        for i, vector in enumerate(vectors)
    ]
    for copy in copies:
        copy.start()
    for copy in copies:
        copy.wait()
    reads = [functools.partial(lambda f, r: kept_ref[f, r], f, r) for f in range(frames) for r in range(rows)]
    line_ref[...] = jnp.broadcast_to(local_moments(reads, channels), line_ref.shape)


def edges_kernel(members, lines_ref, x_ref, prev_ref, line_ref, pair_ref, cross_ref):
    rows = x_ref.shape[1]
    _, _, pair_from, cross_from = places(rows)
    for out_ref, at in ((pair_ref, pair_from), (cross_ref, cross_from)):
        out_ref[0:2] = prev_ref[:, pl.ds(at, 2)]
        out_ref[2:4] = x_ref[:, pl.ds(at, 2)]
    line_ref[...] = jnp.broadcast_to(merged_lines(lines_ref[...], members), line_ref.shape)


def merge_kernel(members, lines_ref, line_ref):
    line_ref[...] = jnp.broadcast_to(merged_lines(lines_ref[...], members), line_ref.shape)


def scaling(lines_ref, params_ref, norm, members):
    channels = params_ref.shape[1]
    devices = lax.axis_size("tm") * lax.axis_size("band")
    line = merged_lines(lines_ref[...], members * lax.axis_size("band"))
    centre, inverse = channel_moments(line, members * devices, channels)
    gain, shift = params_ref[2 * norm : 2 * norm + 1], params_ref[2 * norm + 1 : 2 * norm + 2]
    return centre, 0.5 * inverse * gain, 0.5 * shift


def at_ends():
    band = lax.axis_index("band")
    return lax.axis_index("tm") == 0, band == 0, band == lax.axis_size("band") - 1


def first_kernel(members, x_ref, prev_ref, pair_ref, cross_ref, lines_ref, params_ref, weight_ref,
                 hidden_ref, line_ref, act_ref):
    frames, rows, cols, channels = x_ref.shape
    leading, top, bottom = at_ends()
    even = lax.rem(lax.axis_index("band"), 2) == 0
    norm = scaling(lines_ref, params_ref, 0, members)

    def row_of(f, r):
        inner = prev_ref if f < 2 else x_ref
        if 2 <= r < rows + 2:
            return inner[f % 2, r - 2]
        if r < 2:
            outer = jnp.where(even, cross_ref[f, r], pair_ref[f, r])
            return jnp.where(top, inner[f % 2, 0], outer) if r == 1 else outer
        outer = jnp.where(even, pair_ref[f, r - rows - 2], cross_ref[f, r - rows - 2])
        return jnp.where(bottom, inner[f % 2, rows - 1], outer) if r == rows + 2 else outer

    def activate(f):
        for r in range(rows + 4):
            x = jnp.where(leading, row_of(2, r), row_of(f, r)) if f < 2 else row_of(f, r)
            act_ref[f, r] = activated(x, *norm)

    for f in range(2 + frames):
        activate(f)
    weight_of = lambda k: weight_ref[:, k].reshape(9 * channels, -1)
    for f in range(frames):
        hidden_ref[f] = convolved(act_ref, weight_of, f, 0, rows + 2).astype(jnp.bfloat16)
    reads = [functools.partial(lambda f, r: hidden_ref[f, r + 1], f, r) for f in range(frames) for r in range(rows)]
    line_ref[...] = jnp.broadcast_to(local_moments(reads, channels), line_ref.shape)


def pieces(frames, rows):
    return [(f, 0, rows) for f in range(frames - 1)] + [(frames - 1, 0, rows // 2), (frames - 1, rows // 2, rows // 2)]


def second_kernel(members, hidden_ref, prev_ref, lines_ref, params_ref, x_ref, weight_ref, out_ref,
                  act_ref, made_ref, out_sems):
    frames, rows, cols, channels = x_ref.shape
    leading, top, bottom = at_ends()
    norm = scaling(lines_ref, params_ref, 1, members)

    def row_of(f, r):
        ref = prev_ref if f < 2 else hidden_ref
        if r == 0:
            return jnp.where(top, ref[f % 2, 1], ref[f % 2, 0])
        if r == rows + 1:
            return jnp.where(bottom, ref[f % 2, rows], ref[f % 2, rows + 1])
        return ref[f % 2, r]

    def activate(f):
        for r in range(rows + 2):
            x = jnp.where(leading, row_of(2, r), row_of(f, r)) if f < 2 else row_of(f, r)
            act_ref[f, r] = activated(x, *norm)

    for f in range(2 + frames):
        activate(f)
    weight_of = lambda k: weight_ref[:, k].reshape(9 * channels, -1)
    outs = []
    for f, first, count in pieces(frames, rows):
        at = f, pl.ds(first, count)
        summed = x_ref[at].astype(jnp.float32) + convolved(act_ref, weight_of, f, first, count)
        made_ref[at] = summed.astype(jnp.bfloat16)
        outs.append(pltpu.make_async_copy(made_ref.at[at], out_ref.at[at], out_sems.at[len(outs)]))
        outs[-1].start()
    for copy in outs:
        copy.wait()


def local(
    features, first_gain, first_shift, first_weight, second_gain, second_shift, second_weight
):
    frames, rows, cols, channels = features.shape
    outputs = first_weight.shape[-1]
    tm, band = lax.axis_size("tm"), lax.axis_size("band")
    members = frames * rows * cols * (channels // GROUPS)
    vmem = pl.BlockSpec(memory_space=pltpu.VMEM)
    hbm = pl.BlockSpec(memory_space=pltpu.HBM)
    params = pltpu.CompilerParams(vmem_limit_bytes=VMEM_LIMIT)
    small = pltpu.CompilerParams(vmem_limit_bytes=4 * 1024 * 1024)
    line = lambda count: jax.ShapeDtypeStruct((count, LANES), jnp.float32)
    block = lambda f, r: jax.ShapeDtypeStruct((f, r, cols, channels), jnp.bfloat16)
    held = lambda f, r: pltpu.VMEM((f, r, cols, channels), jnp.bfloat16)
    dmas = lambda count: pltpu.SemaphoreType.DMA((count,))
    taps = lambda weight: weight.reshape(9, 3, channels, outputs)
    stay = lambda value: pltpu.with_memory_space_constraint(value, pltpu.HBM)
    spread_over = lambda lines, axis: lax.all_to_all(lines, axis, 0, 0, tiled=True)
    vectors = [v.reshape(1, channels) for v in (first_gain, first_shift, second_gain, second_shift)]

    prev = next_frames(features)
    lines, kept, vectors = pl.pallas_call(
        stats_kernel,
        out_shape=[line(band), block(frames, rows), jax.ShapeDtypeStruct((8, channels), jnp.float32)],
        in_specs=[hbm] * 5,
        out_specs=[vmem] * 3,
        scratch_shapes=[dmas(frames + 4)],
        compiler_params=small,
        name="moments",
    )(stay(features), *[stay(v) for v in vectors])
    lines = spread_over(lines, "band")
    lines, pair, cross = pl.pallas_call(
        functools.partial(edges_kernel, members),
        out_shape=[line(tm), block(frames + 2, 2), block(frames + 2, 2)],
        in_specs=[vmem] * 3,
        out_specs=[vmem] * 3,
        compiler_params=small,
        cost_estimate=pl.CostEstimate(flops=4 * 10**9, bytes_accessed=0, transcendentals=0),
        name="edges",
    )(lines, kept, prev)
    pair = swapped(pair, "band", 0)
    cross = swapped(cross, "band", 1)
    lines = spread_over(lines, "tm")

    hidden, lines = pl.pallas_call(
        functools.partial(first_kernel, members),
        out_shape=[block(frames, rows + 2), line(band)],
        in_specs=[vmem] * 7,
        out_specs=[vmem, vmem],
        scratch_shapes=[held(frames + 2, rows + 4)],
        compiler_params=params,
        name="first_conv",
    )(kept, prev, pair, cross, lines, vectors, taps(first_weight))

    prev = next_frames(hidden)
    lines = spread_over(lines, "band")
    lines = pl.pallas_call(
        functools.partial(merge_kernel, members),
        out_shape=line(tm),
        in_specs=[vmem],
        out_specs=vmem,
        compiler_params=small,
        name="merge",
    )(lines)
    lines = spread_over(lines, "tm")

    return pl.pallas_call(
        functools.partial(second_kernel, members),
        out_shape=block(frames, rows),
        in_specs=[vmem] * 6,
        out_specs=hbm,
        scratch_shapes=[held(frames + 2, rows + 2), held(frames, rows), dmas(frames + 1)],
        compiler_params=params,
        name="second_conv",
    )(hidden, prev, lines, vectors, kept, taps(second_weight))


def solution(mesh):
    in_specs = (P("tm", "band", None, None), P(), P(), P(), P(), P(), P())
    out_specs = P("tm", "band", None, None)
    return jax.shard_map(local, mesh=mesh, in_specs=in_specs, out_specs=out_specs, check_vma=False)
```

```python
import functools

import jax
import jax.numpy as jnp
from jax import lax
from jax.experimental import pallas as pl
from jax.experimental.pallas import tpu as pltpu
from jax.sharding import PartitionSpec as P

GROUPS = 32
EPSILON = 1e-06
LANES = 128
VMEM_LIMIT = 32 * 1024 * 1024
HIGHEST = lax.Precision.HIGHEST


def next_frames(value):
    count = lax.axis_size("tm")
    return lax.ppermute(value, "tm", [(i, i + 1) for i in range(count - 1)])


def swapped(value, axis, first):
    count = lax.axis_size(axis)
    pairs = []
    for i in range(first, count - 1, 2):
        pairs += [(i, i + 1), (i + 1, i)]
    return lax.ppermute(value, axis, pairs)


def indicator(rows, cols, fn):
    r = lax.broadcasted_iota(jnp.int32, (rows, cols), 0)
    c = lax.broadcasted_iota(jnp.int32, (rows, cols), 1)
    return jnp.where(fn(r, c), 1.0, 0.0).astype(jnp.float32)


def exact_dot(a, b):
    return jnp.dot(a, b, precision=HIGHEST, preferred_element_type=jnp.float32)


def folded(block):
    cols, channels = block.shape
    return jnp.sum(block.reshape(cols // 8, 8, channels), axis=0)


def local_moments(rows, channels):
    size = channels // GROUPS
    total = folded(rows[0]().astype(jnp.float32))
    for row in rows[1:]:
        total = total + folded(row().astype(jnp.float32))
    positions = len(rows) * rows[0]().shape[0]
    channel_mean = jnp.sum(total, axis=0, keepdims=True) * (1.0 / positions)
    channel_mean = jnp.broadcast_to(channel_mean, (8, channels))
    same = indicator(channels, channels, lambda r, c: r // size == c // size)
    group_mean = exact_dot(channel_mean, same) * (1.0 / size)
    centre = group_mean[:1]
    spread = None
    for row in rows:
        off = row().astype(jnp.float32) - centre
        part = folded(off * off)
        spread = part if spread is None else spread + part
    first = indicator(channels, LANES, lambda r, c: r // size == c)
    second = indicator(channels, LANES, lambda r, c: r // size + GROUPS == c)
    spread = jnp.broadcast_to(jnp.sum(spread, axis=0, keepdims=True), (8, channels))
    line = exact_dot(channel_mean, first) * (1.0 / size) + exact_dot(spread, second)
    return line[:1]


def merged_lines(lines, members):
    count = lines.shape[0]
    total = jnp.sum(lines, axis=0, keepdims=True)
    mean = total * (1.0 / count)
    off = lines - mean
    between = jnp.sum(off * off, axis=0, keepdims=True) * members
    lane = lax.broadcasted_iota(jnp.int32, (1, LANES), 1)
    between = jnp.broadcast_to(between, (8, LANES))
    between = pltpu.roll(between, GROUPS, 1)[:1]
    return jnp.where(lane < GROUPS, mean, jnp.where(lane < 2 * GROUPS, total + between, 0.0))


def channel_moments(line, members, channels):
    size = channels // GROUPS
    pick_first = indicator(LANES, channels, lambda r, c: c // size == r)
    pick_second = indicator(LANES, channels, lambda r, c: c // size + GROUPS == r)
    line = jnp.broadcast_to(line, (8, LANES))
    centre = exact_dot(line, pick_first)[:1]
    variance = exact_dot(line, pick_second)[:1] * (1.0 / members)
    return centre, lax.rsqrt(variance + EPSILON)


def activated(x, centre, scale, offset):
    half = (x.astype(jnp.float32) - centre) * scale + offset
    return half + half * jnp.tanh(half)


def mixed_frames(act_ref, row, frames):
    first, second, third, fourth = frames
    for part, value in enumerate((first - third, second + third, third - second, second - fourth)):
        act_ref[part, row] = value.astype(jnp.bfloat16)


def mix_weight(weight_ref, mixed_ref):
    for t in range(9):
        first, middle, last = (weight_ref[3 * i + t // 3, t % 3].astype(jnp.float32) for i in range(3))
        ends = 0.5 * (first + last)
        middle = 0.5 * middle
        mixed_ref[0, t // 3, t % 3] = (ends + middle).astype(jnp.bfloat16)
        mixed_ref[1, t // 3, t % 3] = (ends - middle).astype(jnp.bfloat16)


def convolved(act_ref, weight_ref, mixed_ref, row_count):
    cols, channels = act_ref.shape[2:]
    windows = [
        jnp.concatenate([act_ref[part, j : j + row_count].reshape(row_count * cols, channels) for j in range(3)], axis=-1)
        for part in range(4)
    ]
    early = late = None
    for k in range(3):
        taps = weight_ref[0:3, k], mixed_ref[0, :, k], mixed_ref[1, :, k], weight_ref[6:9, k]
        first, second, third, fourth = (
            jnp.dot(window, tap.reshape(3 * channels, -1), preferred_element_type=jnp.float32).reshape(row_count, cols, -1)
            for window, tap in zip(windows, taps)
        )
        pair = first + second + third, second - third - fourth
        if k != 1:
            column = lax.broadcasted_iota(jnp.int32, first.shape, 1)
            edge, by = (0, 1) if k == 0 else (cols - 1, cols - 1)
            pair = [jnp.where(column == edge, value, pltpu.roll(value, by, 1)) for value in pair]
        early = pair[0] if early is None else early + pair[0]
        late = pair[1] if late is None else late + pair[1]
    return early, late


def places(rows):
    even = lax.rem(lax.axis_index("band"), 2) == 0
    pair_at, cross_at = jnp.where(even, rows + 2, 0), jnp.where(even, 0, rows + 2)
    pair_from, cross_from = jnp.where(even, rows - 2, 0), jnp.where(even, 0, rows - 2)
    return pair_at, cross_at, pair_from, cross_from


def stats_kernel(x_ref, *refs):
    vectors, (line_ref, kept_ref, params_ref, sems) = refs[:4], refs[4:]
    frames, rows, _, channels = x_ref.shape
    copies = [pltpu.make_async_copy(x_ref.at[f], kept_ref.at[f], sems.at[f]) for f in range(frames)]
    copies += [
        pltpu.make_async_copy(vector, params_ref.at[pl.ds(i, 1)], sems.at[frames + i])
        for i, vector in enumerate(vectors)
    ]
    for copy in copies:
        copy.start()
    for copy in copies:
        copy.wait()
    reads = [functools.partial(lambda f, r: kept_ref[f, r], f, r) for f in range(frames) for r in range(rows)]
    line_ref[...] = jnp.broadcast_to(local_moments(reads, channels), line_ref.shape)


def edges_kernel(members, lines_ref, x_ref, prev_ref, line_ref, pair_ref, cross_ref):
    rows = x_ref.shape[1]
    _, _, pair_from, cross_from = places(rows)
    for out_ref, at in ((pair_ref, pair_from), (cross_ref, cross_from)):
        out_ref[0:2] = prev_ref[:, pl.ds(at, 2)]
        out_ref[2:4] = x_ref[:, pl.ds(at, 2)]
    line_ref[...] = jnp.broadcast_to(merged_lines(lines_ref[...], members), line_ref.shape)


def merge_kernel(members, lines_ref, line_ref):
    line_ref[...] = jnp.broadcast_to(merged_lines(lines_ref[...], members), line_ref.shape)


def scaling(lines_ref, params_ref, norm, members):
    channels = params_ref.shape[1]
    devices = lax.axis_size("tm") * lax.axis_size("band")
    line = merged_lines(lines_ref[...], members * lax.axis_size("band"))
    centre, inverse = channel_moments(line, members * devices, channels)
    gain, shift = params_ref[2 * norm : 2 * norm + 1], params_ref[2 * norm + 1 : 2 * norm + 2]
    return centre, 0.5 * inverse * gain, 0.5 * shift


def at_ends():
    band = lax.axis_index("band")
    return lax.axis_index("tm") == 0, band == 0, band == lax.axis_size("band") - 1


def first_kernel(members, x_ref, prev_ref, pair_ref, cross_ref, lines_ref, params_ref, weight_ref,
                 hidden_ref, line_ref, act_ref, mixed_ref):
    frames, rows, cols, channels = x_ref.shape
    leading, top, bottom = at_ends()
    even = lax.rem(lax.axis_index("band"), 2) == 0
    norm = scaling(lines_ref, params_ref, 0, members)

    def row_of(f, r):
        inner = prev_ref if f < 2 else x_ref
        if 2 <= r < rows + 2:
            return inner[f % 2, r - 2]
        if r < 2:
            outer = jnp.where(even, cross_ref[f, r], pair_ref[f, r])
            return jnp.where(top, inner[f % 2, 0], outer) if r == 1 else outer
        outer = jnp.where(even, pair_ref[f, r - rows - 2], cross_ref[f, r - rows - 2])
        return jnp.where(bottom, inner[f % 2, rows - 1], outer) if r == rows + 2 else outer

    for r in range(rows + 4):
        own = [row_of(f, r) for f in (2, 3)]
        before = [jnp.where(leading, own[0], row_of(f, r)) for f in (0, 1)]
        mixed_frames(act_ref, r, [activated(x, *norm) for x in before + own])
    mix_weight(weight_ref, mixed_ref)
    for f, value in enumerate(convolved(act_ref, weight_ref, mixed_ref, rows + 2)):
        hidden_ref[f] = value.astype(jnp.bfloat16)
    reads = [functools.partial(lambda f, r: hidden_ref[f, r + 1], f, r) for f in range(frames) for r in range(rows)]
    line_ref[...] = jnp.broadcast_to(local_moments(reads, channels), line_ref.shape)


def second_kernel(members, hidden_ref, prev_ref, lines_ref, params_ref, x_ref, weight_ref, out_ref,
                  act_ref, mixed_ref, made_ref, out_sems):
    frames, rows, cols, channels = x_ref.shape
    leading, top, bottom = at_ends()
    norm = scaling(lines_ref, params_ref, 1, members)

    def row_of(f, r):
        ref = prev_ref if f < 2 else hidden_ref
        if r == 0:
            return jnp.where(top, ref[f % 2, 1], ref[f % 2, 0])
        if r == rows + 1:
            return jnp.where(bottom, ref[f % 2, rows], ref[f % 2, rows + 1])
        return ref[f % 2, r]

    for r in range(rows + 2):
        own = [row_of(f, r) for f in (2, 3)]
        before = [jnp.where(leading, own[0], row_of(f, r)) for f in (0, 1)]
        mixed_frames(act_ref, r, [activated(x, *norm) for x in before + own])
    mix_weight(weight_ref, mixed_ref)
    outs = []
    for f, value in enumerate(convolved(act_ref, weight_ref, mixed_ref, rows)):
        made_ref[f] = (x_ref[f].astype(jnp.float32) + value).astype(jnp.bfloat16)
        outs.append(pltpu.make_async_copy(made_ref.at[f], out_ref.at[f], out_sems.at[f]))
        outs[-1].start()
    for copy in outs:
        copy.wait()


def local(
    features, first_gain, first_shift, first_weight, second_gain, second_shift, second_weight
):
    frames, rows, cols, channels = features.shape
    outputs = first_weight.shape[-1]
    tm, band = lax.axis_size("tm"), lax.axis_size("band")
    members = frames * rows * cols * (channels // GROUPS)
    vmem = pl.BlockSpec(memory_space=pltpu.VMEM)
    hbm = pl.BlockSpec(memory_space=pltpu.HBM)
    params = pltpu.CompilerParams(vmem_limit_bytes=VMEM_LIMIT)
    small = pltpu.CompilerParams(vmem_limit_bytes=4 * 1024 * 1024)
    line = lambda count: jax.ShapeDtypeStruct((count, LANES), jnp.float32)
    block = lambda f, r: jax.ShapeDtypeStruct((f, r, cols, channels), jnp.bfloat16)
    held = lambda f, r: pltpu.VMEM((f, r, cols, channels), jnp.bfloat16)
    dmas = lambda count: pltpu.SemaphoreType.DMA((count,))
    taps = lambda weight: weight.reshape(9, 3, channels, outputs)
    mixed = pltpu.VMEM((2, 3, 3, channels, outputs), jnp.bfloat16)
    stay = lambda value: pltpu.with_memory_space_constraint(value, pltpu.HBM)
    spread_over = lambda lines, axis: lax.all_to_all(lines, axis, 0, 0, tiled=True)
    vectors = [v.reshape(1, channels) for v in (first_gain, first_shift, second_gain, second_shift)]

    prev = next_frames(features)
    lines, kept, vectors = pl.pallas_call(
        stats_kernel,
        out_shape=[line(band), block(frames, rows), jax.ShapeDtypeStruct((8, channels), jnp.float32)],
        in_specs=[hbm] * 5,
        out_specs=[vmem] * 3,
        scratch_shapes=[dmas(frames + 4)],
        compiler_params=small,
        name="moments",
    )(stay(features), *[stay(v) for v in vectors])
    lines = spread_over(lines, "band")
    lines, pair, cross = pl.pallas_call(
        functools.partial(edges_kernel, members),
        out_shape=[line(tm), block(frames + 2, 2), block(frames + 2, 2)],
        in_specs=[vmem] * 3,
        out_specs=[vmem] * 3,
        compiler_params=small,
        cost_estimate=pl.CostEstimate(flops=4 * 10**9, bytes_accessed=0, transcendentals=0),
        name="edges",
    )(lines, kept, prev)
    pair = swapped(pair, "band", 0)
    cross = swapped(cross, "band", 1)
    lines = spread_over(lines, "tm")

    hidden, lines = pl.pallas_call(
        functools.partial(first_kernel, members),
        out_shape=[block(frames, rows + 2), line(band)],
        in_specs=[vmem] * 7,
        out_specs=[vmem, vmem],
        scratch_shapes=[held(4, rows + 4), mixed],
        compiler_params=params,
        name="first_conv",
    )(kept, prev, pair, cross, lines, vectors, taps(first_weight))

    prev = next_frames(hidden)
    lines = spread_over(lines, "band")
    lines = pl.pallas_call(
        functools.partial(merge_kernel, members),
        out_shape=line(tm),
        in_specs=[vmem],
        out_specs=vmem,
        compiler_params=small,
        name="merge",
    )(lines)
    lines = spread_over(lines, "tm")

    return pl.pallas_call(
        functools.partial(second_kernel, members),
        out_shape=block(frames, rows),
        in_specs=[vmem] * 6,
        out_specs=hbm,
        scratch_shapes=[held(4, rows + 2), mixed, held(frames, rows), dmas(frames)],
        compiler_params=params,
        name="second_conv",
    )(hidden, prev, lines, vectors, kept, taps(second_weight))


def solution(mesh):
    in_specs = (P("tm", "band", None, None), P(), P(), P(), P(), P(), P())
    out_specs = P("tm", "band", None, None)
    return jax.shard_map(local, mesh=mesh, in_specs=in_specs, out_specs=out_specs, check_vma=False)
```

```python
import functools

import jax
import jax.numpy as jnp
from jax import lax
from jax.experimental import pallas as pl
from jax.experimental.pallas import tpu as pltpu
from jax.sharding import PartitionSpec as P

GROUPS = 32
EPSILON = 1e-06
LANES = 128
VMEM_LIMIT = 32 * 1024 * 1024


def next_frames(value):
    count = lax.axis_size("tm")
    return lax.ppermute(value, "tm", [(i, i + 1) for i in range(count - 1)])


def swapped(value, axis, first):
    count = lax.axis_size(axis)
    pairs = []
    for i in range(first, count - 1, 2):
        pairs += [(i, i + 1), (i + 1, i)]
    return lax.ppermute(value, axis, pairs)


def indicator(rows, cols, fn):
    r = lax.broadcasted_iota(jnp.int32, (rows, cols), 0)
    c = lax.broadcasted_iota(jnp.int32, (rows, cols), 1)
    return jnp.where(fn(r, c), 1.0, 0.0).astype(jnp.bfloat16)


def picked(line, pick):
    parts = []
    for _ in range(3):
        parts.append(line.astype(jnp.bfloat16).astype(jnp.float32))
        line = line - parts[-1]
    row = lax.broadcasted_iota(jnp.int32, (16, line.shape[1]), 0)
    stacked = jnp.where(row == 0, parts[0], jnp.where(row == 1, parts[1], jnp.where(row == 2, parts[2], 0.0)))
    product = jnp.dot(stacked.astype(jnp.bfloat16), pick, preferred_element_type=jnp.float32)
    return jnp.sum(product, axis=0, keepdims=True)


def folded(block):
    cols, channels = block.shape
    return jnp.sum(block.reshape(cols // 8, 8, channels), axis=0)


def local_moments(rows, channels):
    size = channels // GROUPS
    same = indicator(channels, channels, lambda r, c: r // size == c // size)
    first = indicator(channels, LANES, lambda r, c: r // size == c)
    second = indicator(channels, LANES, lambda r, c: r // size + GROUPS == c)
    total = folded(rows[0]().astype(jnp.float32))
    for row in rows[1:]:
        total = total + folded(row().astype(jnp.float32))
    positions = len(rows) * rows[0]().shape[0]
    centre = jnp.sum(total, axis=0, keepdims=True) * (1.0 / positions)
    spread = None
    for row in rows:
        off = row().astype(jnp.float32) - centre
        part = folded(off * off)
        spread = part if spread is None else spread + part
    apart = centre - picked(centre, same) * (1.0 / size)
    spread = jnp.sum(spread, axis=0, keepdims=True) + positions * apart * apart
    return picked(centre, first) * (1.0 / size) + picked(spread, second)


def merged_lines(lines, members):
    count = lines.shape[0]
    total = jnp.sum(lines, axis=0, keepdims=True)
    mean = total * (1.0 / count)
    off = lines - mean
    between = jnp.sum(off * off, axis=0, keepdims=True) * members
    lane = lax.broadcasted_iota(jnp.int32, (1, LANES), 1)
    between = jnp.broadcast_to(between, (8, LANES))
    between = pltpu.roll(between, GROUPS, 1)[:1]
    return jnp.where(lane < GROUPS, mean, jnp.where(lane < 2 * GROUPS, total + between, 0.0))


def channel_moments(line, members, channels):
    size = channels // GROUPS
    pick = indicator(LANES, 2 * channels, lambda r, c: c // size == r)
    wide = picked(line, pick)
    centre, variance = wide[:, :channels], wide[:, channels:] * (1.0 / members)
    return centre, lax.rsqrt(variance + EPSILON)


def activated(x, centre, scale, offset):
    half = (x.astype(jnp.float32) - centre) * scale + offset
    return half + half * jnp.tanh(half)


def mixed_frames(act_ref, row, frames):
    first, second, third, fourth = frames
    for part, value in enumerate((first - third, second + third, third - second, second - fourth)):
        act_ref[part, row] = value.astype(jnp.bfloat16)


def mix_weight(weight_ref, mixed_ref):
    for t in range(9):
        first, middle, last = (weight_ref[3 * i + t // 3, t % 3].astype(jnp.float32) for i in range(3))
        ends = 0.5 * (first + last)
        middle = 0.5 * middle
        mixed_ref[0, t // 3, t % 3] = (ends + middle).astype(jnp.bfloat16)
        mixed_ref[1, t // 3, t % 3] = (ends - middle).astype(jnp.bfloat16)


def convolved(act_ref, weight_ref, mixed_ref, row_count):
    cols, channels = act_ref.shape[2:]
    windows = [
        jnp.concatenate([act_ref[part, j : j + row_count].reshape(row_count * cols, channels) for j in range(3)], axis=-1)
        for part in range(4)
    ]
    early = late = None
    for k in range(3):
        taps = weight_ref[0:3, k], mixed_ref[0, :, k], mixed_ref[1, :, k], weight_ref[6:9, k]
        first, second, third, fourth = (
            jnp.dot(window, tap.reshape(3 * channels, -1), preferred_element_type=jnp.float32).reshape(row_count, cols, -1)
            for window, tap in zip(windows, taps)
        )
        pair = first + second + third, second - third - fourth
        if k != 1:
            column = lax.broadcasted_iota(jnp.int32, first.shape, 1)
            edge, by = (0, 1) if k == 0 else (cols - 1, cols - 1)
            pair = [jnp.where(column == edge, value, pltpu.roll(value, by, 1)) for value in pair]
        early = pair[0] if early is None else early + pair[0]
        late = pair[1] if late is None else late + pair[1]
    return early, late


def places(rows):
    even = lax.rem(lax.axis_index("band"), 2) == 0
    pair_at, cross_at = jnp.where(even, rows + 2, 0), jnp.where(even, 0, rows + 2)
    pair_from, cross_from = jnp.where(even, rows - 2, 0), jnp.where(even, 0, rows - 2)
    return pair_at, cross_at, pair_from, cross_from


def stats_kernel(x_ref, *refs):
    vectors, (line_ref, kept_ref, params_ref, sems) = refs[:4], refs[4:]
    frames, rows, _, channels = x_ref.shape
    copies = [pltpu.make_async_copy(x_ref.at[f], kept_ref.at[f], sems.at[f]) for f in range(frames)]
    copies += [
        pltpu.make_async_copy(vector, params_ref.at[pl.ds(i, 1)], sems.at[frames + i])
        for i, vector in enumerate(vectors)
    ]
    for copy in copies:
        copy.start()
    for copy in copies:
        copy.wait()
    reads = [functools.partial(lambda f, r: kept_ref[f, r], f, r) for f in range(frames) for r in range(rows)]
    line_ref[...] = jnp.broadcast_to(local_moments(reads, channels), line_ref.shape)


def edges_kernel(members, lines_ref, x_ref, prev_ref, line_ref, pair_ref, cross_ref):
    rows = x_ref.shape[1]
    _, _, pair_from, cross_from = places(rows)
    for out_ref, at in ((pair_ref, pair_from), (cross_ref, cross_from)):
        out_ref[0:2] = prev_ref[:, pl.ds(at, 2)]
        out_ref[2:4] = x_ref[:, pl.ds(at, 2)]
    line_ref[...] = jnp.broadcast_to(merged_lines(lines_ref[...], members), line_ref.shape)


def ring_merge_kernel(members, a_ref, b_ref, c_ref, d_ref, block_ref, line_ref, sent_ref):
    lines = jnp.concatenate([r[0:1] for r in (a_ref, b_ref, c_ref, d_ref)], axis=0)
    line_ref[...] = jnp.broadcast_to(merged_lines(lines, members), line_ref.shape)


def merge_kernel(members, lines_ref, line_ref):
    line_ref[...] = jnp.broadcast_to(merged_lines(lines_ref[...], members), line_ref.shape)


def scaling(lines_ref, params_ref, norm, members):
    channels = params_ref.shape[1]
    devices = lax.axis_size("tm") * lax.axis_size("band")
    line = merged_lines(lines_ref[...], members * devices // lines_ref.shape[0])
    centre, inverse = channel_moments(line, members * devices, channels)
    gain, shift = params_ref[2 * norm : 2 * norm + 1], params_ref[2 * norm + 1 : 2 * norm + 2]
    return centre, 0.5 * inverse * gain, 0.5 * shift


def at_ends():
    band = lax.axis_index("band")
    return lax.axis_index("tm") == 0, band == 0, band == lax.axis_size("band") - 1


def first_kernel(members, x_ref, prev_ref, pair_ref, cross_ref, lines_ref, params_ref, weight_ref,
                 hidden_ref, line_ref, act_ref, mixed_ref):
    frames, rows, cols, channels = x_ref.shape
    leading, top, bottom = at_ends()
    even = lax.rem(lax.axis_index("band"), 2) == 0
    norm = scaling(lines_ref, params_ref, 0, members)

    def row_of(f, r):
        inner = prev_ref if f < 2 else x_ref
        if 2 <= r < rows + 2:
            return inner[f % 2, r - 2]
        if r < 2:
            outer = jnp.where(even, cross_ref[f, r], pair_ref[f, r])
            return jnp.where(top, inner[f % 2, 0], outer) if r == 1 else outer
        outer = jnp.where(even, pair_ref[f, r - rows - 2], cross_ref[f, r - rows - 2])
        return jnp.where(bottom, inner[f % 2, rows - 1], outer) if r == rows + 2 else outer

    for r in range(rows + 4):
        own = [row_of(f, r) for f in (2, 3)]
        before = [jnp.where(leading, own[0], row_of(f, r)) for f in (0, 1)]
        mixed_frames(act_ref, r, [activated(x, *norm) for x in before + own])
    mix_weight(weight_ref, mixed_ref)
    for f, value in enumerate(convolved(act_ref, weight_ref, mixed_ref, rows + 2)):
        hidden_ref[f] = value.astype(jnp.bfloat16)
    reads = [functools.partial(lambda f, r: hidden_ref[f, r + 1], f, r) for f in range(frames) for r in range(rows)]
    line_ref[...] = jnp.broadcast_to(local_moments(reads, channels), line_ref.shape)


def second_kernel(members, hidden_ref, prev_ref, lines_ref, params_ref, x_ref, weight_ref, out_ref,
                  act_ref, mixed_ref, made_ref, out_sems):
    frames, rows, cols, channels = x_ref.shape
    leading, top, bottom = at_ends()
    norm = scaling(lines_ref, params_ref, 1, members)

    def row_of(f, r):
        ref = prev_ref if f < 2 else hidden_ref
        if r == 0:
            return jnp.where(top, ref[f % 2, 1], ref[f % 2, 0])
        if r == rows + 1:
            return jnp.where(bottom, ref[f % 2, rows], ref[f % 2, rows + 1])
        return ref[f % 2, r]

    for r in range(rows + 2):
        own = [row_of(f, r) for f in (2, 3)]
        before = [jnp.where(leading, own[0], row_of(f, r)) for f in (0, 1)]
        mixed_frames(act_ref, r, [activated(x, *norm) for x in before + own])
    mix_weight(weight_ref, mixed_ref)
    outs = []
    for f, value in enumerate(convolved(act_ref, weight_ref, mixed_ref, rows)):
        made_ref[f] = (x_ref[f].astype(jnp.float32) + value).astype(jnp.bfloat16)
        outs.append(pltpu.make_async_copy(made_ref.at[f], out_ref.at[f], out_sems.at[f]))
        outs[-1].start()
    for copy in outs:
        copy.wait()


def local(
    features, first_gain, first_shift, first_weight, second_gain, second_shift, second_weight
):
    frames, rows, cols, channels = features.shape
    outputs = first_weight.shape[-1]
    tm, band = lax.axis_size("tm"), lax.axis_size("band")
    members = frames * rows * cols * (channels // GROUPS)
    vmem = pl.BlockSpec(memory_space=pltpu.VMEM)
    hbm = pl.BlockSpec(memory_space=pltpu.HBM)
    anywhere = pl.BlockSpec(memory_space=pl.ANY)
    params = pltpu.CompilerParams(vmem_limit_bytes=VMEM_LIMIT)
    small = pltpu.CompilerParams(vmem_limit_bytes=4 * 1024 * 1024)
    line = lambda count: jax.ShapeDtypeStruct((count, LANES), jnp.float32)
    block = lambda f, r: jax.ShapeDtypeStruct((f, r, cols, channels), jnp.bfloat16)
    held = lambda f, r: pltpu.VMEM((f, r, cols, channels), jnp.bfloat16)
    dmas = lambda count: pltpu.SemaphoreType.DMA((count,))
    taps = lambda weight: weight.reshape(9, 3, channels, outputs)
    mixed = pltpu.VMEM((2, 3, 3, channels, outputs), jnp.bfloat16)
    stay = lambda value: pltpu.with_memory_space_constraint(value, pltpu.HBM)
    spread_over = lambda lines, axis: lax.all_to_all(lines, axis, 0, 0, tiled=True)
    vectors = [v.reshape(1, channels) for v in (first_gain, first_shift, second_gain, second_shift)]

    prev = next_frames(features)
    lines, kept, vectors = pl.pallas_call(
        stats_kernel,
        out_shape=[line(band), block(frames, rows), jax.ShapeDtypeStruct((8, channels), jnp.float32)],
        in_specs=[hbm] * 5,
        out_specs=[vmem] * 3,
        scratch_shapes=[dmas(frames + 4)],
        compiler_params=small,
        name="moments",
    )(stay(features), *[stay(v) for v in vectors])
    lines = spread_over(lines, "band")
    lines, pair, cross = pl.pallas_call(
        functools.partial(edges_kernel, members),
        out_shape=[line(tm), block(frames + 2, 2), block(frames + 2, 2)],
        in_specs=[vmem] * 3,
        out_specs=[vmem] * 3,
        compiler_params=small,
        cost_estimate=pl.CostEstimate(flops=4 * 10**9, bytes_accessed=0, transcendentals=0),
        name="edges",
    )(lines, kept, prev)
    pair = swapped(pair, "band", 0)
    cross = swapped(cross, "band", 1)
    lines = spread_over(lines, "tm")

    hidden, lines = pl.pallas_call(
        functools.partial(first_kernel, members),
        out_shape=[block(frames, rows + 2), line(8)],
        in_specs=[vmem] * 7,
        out_specs=[vmem, vmem],
        scratch_shapes=[held(4, rows + 4), mixed],
        compiler_params=params,
        name="first_conv",
    )(kept, prev, pair, cross, lines, vectors, taps(first_weight))

    xz = [[(4 * x + y) * band + b for x in range(4) for b in range(band)] for y in range(4)]
    def rot(v, by):
        return lax.ppermute(v, "tm", [(i, i - i % 4 + (i + by) % 4) for i in range(tm)])
    got = [rot(lines, by) for by in (2, 1, 3)]
    lines, hidden = pl.pallas_call(
        functools.partial(ring_merge_kernel, members),
        out_shape=[line(64), block(frames, rows + 2)],
        in_specs=[vmem] * 4 + [anywhere],
        out_specs=[vmem, anywhere],
        input_output_aliases={4: 1},
        compiler_params=small,
        name="merge",
    )(lines, *got, hidden)
    prev = next_frames(hidden)
    lines = lax.all_to_all(lines, ("tm", "band"), 0, 0, tiled=True, axis_index_groups=xz)

    return pl.pallas_call(
        functools.partial(second_kernel, members),
        out_shape=block(frames, rows),
        in_specs=[vmem] * 6,
        out_specs=hbm,
        scratch_shapes=[held(4, rows + 2), mixed, held(frames, rows), dmas(frames)],
        compiler_params=params,
        name="second_conv",
    )(hidden, prev, lines, vectors, kept, taps(second_weight))


def solution(mesh):
    in_specs = (P("tm", "band", None, None), P(), P(), P(), P(), P(), P())
    out_specs = P("tm", "band", None, None)
    return jax.shard_map(local, mesh=mesh, in_specs=in_specs, out_specs=out_specs, check_vma=False)
```

```python
import functools

import jax
import jax.numpy as jnp
from jax import lax
from jax.experimental import pallas as pl
from jax.experimental.pallas import tpu as pltpu
from jax.sharding import PartitionSpec as P

GROUPS = 32
EPSILON = 1e-06
LANES = 128
VMEM_LIMIT = 32 * 1024 * 1024


def next_frames(value):
    count = lax.axis_size("tm")
    return lax.ppermute(value, "tm", [(i, i + 1) for i in range(count - 1)])


def swapped(value, axis, first):
    count = lax.axis_size(axis)
    pairs = []
    for i in range(first, count - 1, 2):
        pairs += [(i, i + 1), (i + 1, i)]
    return lax.ppermute(value, axis, pairs)


def indicator(rows, cols, fn):
    r = lax.broadcasted_iota(jnp.int32, (rows, cols), 0)
    c = lax.broadcasted_iota(jnp.int32, (rows, cols), 1)
    return jnp.where(fn(r, c), 1.0, 0.0).astype(jnp.bfloat16)


def picked(line, pick):
    parts = []
    for _ in range(3):
        parts.append(line.astype(jnp.bfloat16).astype(jnp.float32))
        line = line - parts[-1]
    row = lax.broadcasted_iota(jnp.int32, (16, line.shape[1]), 0)
    stacked = jnp.where(row == 0, parts[0], jnp.where(row == 1, parts[1], jnp.where(row == 2, parts[2], 0.0)))
    product = jnp.dot(stacked.astype(jnp.bfloat16), pick, preferred_element_type=jnp.float32)
    return jnp.sum(product, axis=0, keepdims=True)


def folded(block):
    cols, channels = block.shape
    return jnp.sum(block.reshape(cols // 8, 8, channels), axis=0)


def local_moments(rows, channels):
    size = channels // GROUPS
    same = indicator(channels, channels, lambda r, c: r // size == c // size)
    first = indicator(channels, LANES, lambda r, c: r // size == c)
    second = indicator(channels, LANES, lambda r, c: r // size + GROUPS == c)
    total = folded(rows[0]().astype(jnp.float32))
    for row in rows[1:]:
        total = total + folded(row().astype(jnp.float32))
    positions = len(rows) * rows[0]().shape[0]
    centre = jnp.sum(total, axis=0, keepdims=True) * (1.0 / positions)
    spread = None
    for row in rows:
        off = row().astype(jnp.float32) - centre
        part = folded(off * off)
        spread = part if spread is None else spread + part
    apart = centre - picked(centre, same) * (1.0 / size)
    spread = jnp.sum(spread, axis=0, keepdims=True) + positions * apart * apart
    return picked(centre, first) * (1.0 / size) + picked(spread, second)


def merged_lines(lines, members):
    count = lines.shape[0]
    total = jnp.sum(lines, axis=0, keepdims=True)
    mean = total * (1.0 / count)
    off = lines - mean
    between = jnp.sum(off * off, axis=0, keepdims=True) * members
    lane = lax.broadcasted_iota(jnp.int32, (1, LANES), 1)
    between = jnp.broadcast_to(between, (8, LANES))
    between = pltpu.roll(between, GROUPS, 1)[:1]
    return jnp.where(lane < GROUPS, mean, jnp.where(lane < 2 * GROUPS, total + between, 0.0))


def channel_moments(line, members, channels):
    size = channels // GROUPS
    pick = indicator(LANES, 2 * channels, lambda r, c: c // size == r)
    wide = picked(line, pick)
    centre, variance = wide[:, :channels], wide[:, channels:] * (1.0 / members)
    return centre, lax.rsqrt(variance + EPSILON)


def activated(x, centre, scale, offset):
    half = (x.astype(jnp.float32) - centre) * scale + offset
    return half + half * jnp.tanh(half)


def mixed_frames(act_ref, row, frames):
    first, second, third, fourth = frames
    for part, value in enumerate((first - third, second + third, third - second, second - fourth)):
        act_ref[part, row] = value.astype(jnp.bfloat16)


def mix_weight(weight_ref, mixed_ref):
    for t in range(9):
        first, middle, last = (weight_ref[3 * i + t // 3, t % 3].astype(jnp.float32) for i in range(3))
        ends = 0.5 * (first + last)
        middle = 0.5 * middle
        mixed_ref[0, t // 3, t % 3] = (ends + middle).astype(jnp.bfloat16)
        mixed_ref[1, t // 3, t % 3] = (ends - middle).astype(jnp.bfloat16)


def convolved(act_ref, weight_ref, mixed_ref, row_count):
    cols, channels = act_ref.shape[2:]
    windows = [
        jnp.concatenate([act_ref[part, j : j + row_count].reshape(row_count * cols, channels) for j in range(3)], axis=-1)
        for part in range(4)
    ]
    early = late = None
    for k in range(3):
        taps = weight_ref[0:3, k], mixed_ref[0, :, k], mixed_ref[1, :, k], weight_ref[6:9, k]
        first, second, third, fourth = (
            jnp.dot(window, tap.reshape(3 * channels, -1), preferred_element_type=jnp.float32).reshape(row_count, cols, -1)
            for window, tap in zip(windows, taps)
        )
        pair = first + second + third, second - third - fourth
        if k != 1:
            column = lax.broadcasted_iota(jnp.int32, first.shape, 1)
            edge, by = (0, 1) if k == 0 else (cols - 1, cols - 1)
            pair = [jnp.where(column == edge, value, pltpu.roll(value, by, 1)) for value in pair]
        early = pair[0] if early is None else early + pair[0]
        late = pair[1] if late is None else late + pair[1]
    return early, late


def places(rows):
    even = lax.rem(lax.axis_index("band"), 2) == 0
    pair_at, cross_at = jnp.where(even, rows + 2, 0), jnp.where(even, 0, rows + 2)
    pair_from, cross_from = jnp.where(even, rows - 2, 0), jnp.where(even, 0, rows - 2)
    return pair_at, cross_at, pair_from, cross_from


def stats_kernel(x_ref, *refs):
    vectors, (line_ref, kept_ref, params_ref, sems) = refs[:4], refs[4:]
    frames, rows, _, channels = x_ref.shape
    copies = [pltpu.make_async_copy(x_ref.at[f], kept_ref.at[f], sems.at[f]) for f in range(frames)]
    copies += [
        pltpu.make_async_copy(vector, params_ref.at[pl.ds(i, 1)], sems.at[frames + i])
        for i, vector in enumerate(vectors)
    ]
    for copy in copies:
        copy.start()
    for copy in copies:
        copy.wait()
    reads = [functools.partial(lambda f, r: kept_ref[f, r], f, r) for f in range(frames) for r in range(rows)]
    line_ref[...] = jnp.broadcast_to(local_moments(reads, channels), line_ref.shape)


def edges_kernel(members, lines_ref, x_ref, prev_ref, line_ref, pair_ref, cross_ref):
    rows = x_ref.shape[1]
    _, _, pair_from, cross_from = places(rows)
    for out_ref, at in ((pair_ref, pair_from), (cross_ref, cross_from)):
        out_ref[0:2] = prev_ref[:, pl.ds(at, 2)]
        out_ref[2:4] = x_ref[:, pl.ds(at, 2)]
    line_ref[...] = jnp.broadcast_to(merged_lines(lines_ref[...], members), line_ref.shape)


def ring_merge_kernel(members, a_ref, b_ref, c_ref, d_ref, line_ref):
    lines = jnp.concatenate([r[0:1] for r in (a_ref, b_ref, c_ref, d_ref)], axis=0)
    line_ref[...] = jnp.broadcast_to(merged_lines(lines, members), line_ref.shape)


def merge_kernel(members, lines_ref, line_ref):
    line_ref[...] = jnp.broadcast_to(merged_lines(lines_ref[...], members), line_ref.shape)


def scaling(lines_ref, params_ref, norm, members):
    channels = params_ref.shape[1]
    devices = lax.axis_size("tm") * lax.axis_size("band")
    line = merged_lines(lines_ref[...], members * devices // lines_ref.shape[0])
    centre, inverse = channel_moments(line, members * devices, channels)
    gain, shift = params_ref[2 * norm : 2 * norm + 1], params_ref[2 * norm + 1 : 2 * norm + 2]
    return centre, 0.5 * inverse * gain, 0.5 * shift


def at_ends():
    band = lax.axis_index("band")
    return lax.axis_index("tm") == 0, band == 0, band == lax.axis_size("band") - 1


def first_kernel(members, x_ref, prev_ref, pair_ref, cross_ref, lines_ref, params_ref, weight_ref,
                 hidden_ref, line_ref, act_ref, mixed_ref):
    frames, rows, cols, channels = x_ref.shape
    leading, top, bottom = at_ends()
    even = lax.rem(lax.axis_index("band"), 2) == 0
    norm = scaling(lines_ref, params_ref, 0, members)

    def row_of(f, r):
        inner = prev_ref if f < 2 else x_ref
        if 2 <= r < rows + 2:
            return inner[f % 2, r - 2]
        if r < 2:
            outer = jnp.where(even, cross_ref[f, r], pair_ref[f, r])
            return jnp.where(top, inner[f % 2, 0], outer) if r == 1 else outer
        outer = jnp.where(even, pair_ref[f, r - rows - 2], cross_ref[f, r - rows - 2])
        return jnp.where(bottom, inner[f % 2, rows - 1], outer) if r == rows + 2 else outer

    for r in range(rows + 4):
        own = [row_of(f, r) for f in (2, 3)]
        before = [jnp.where(leading, own[0], row_of(f, r)) for f in (0, 1)]
        mixed_frames(act_ref, r, [activated(x, *norm) for x in before + own])
    mix_weight(weight_ref, mixed_ref)
    for f, value in enumerate(convolved(act_ref, weight_ref, mixed_ref, rows + 2)):
        hidden_ref[f] = value.astype(jnp.bfloat16)
    reads = [functools.partial(lambda f, r: hidden_ref[f, r + 1], f, r) for f in range(frames) for r in range(rows)]
    line_ref[...] = jnp.broadcast_to(local_moments(reads, channels), line_ref.shape)


def second_kernel(members, hidden_ref, prev_ref, lines_ref, params_ref, x_ref, weight_ref, out_ref,
                  act_ref, mixed_ref, made_ref, out_sems):
    frames, rows, cols, channels = x_ref.shape
    leading, top, bottom = at_ends()
    norm = scaling(lines_ref, params_ref, 1, members)

    def row_of(f, r):
        ref = prev_ref if f < 2 else hidden_ref
        if r == 0:
            return jnp.where(top, ref[f % 2, 1], ref[f % 2, 0])
        if r == rows + 1:
            return jnp.where(bottom, ref[f % 2, rows], ref[f % 2, rows + 1])
        return ref[f % 2, r]

    for r in range(rows + 2):
        own = [row_of(f, r) for f in (2, 3)]
        before = [jnp.where(leading, own[0], row_of(f, r)) for f in (0, 1)]
        mixed_frames(act_ref, r, [activated(x, *norm) for x in before + own])
    mix_weight(weight_ref, mixed_ref)
    outs = []
    for f, value in enumerate(convolved(act_ref, weight_ref, mixed_ref, rows)):
        made_ref[f] = (x_ref[f].astype(jnp.float32) + value).astype(jnp.bfloat16)
        outs.append(pltpu.make_async_copy(made_ref.at[f], out_ref.at[f], out_sems.at[f]))
        outs[-1].start()
    for copy in outs:
        copy.wait()


def local(
    features, first_gain, first_shift, first_weight, second_gain, second_shift, second_weight
):
    frames, rows, cols, channels = features.shape
    outputs = first_weight.shape[-1]
    tm, band = lax.axis_size("tm"), lax.axis_size("band")
    members = frames * rows * cols * (channels // GROUPS)
    vmem = pl.BlockSpec(memory_space=pltpu.VMEM)
    hbm = pl.BlockSpec(memory_space=pltpu.HBM)
    anywhere = pl.BlockSpec(memory_space=pl.ANY)
    params = pltpu.CompilerParams(vmem_limit_bytes=VMEM_LIMIT)
    small = pltpu.CompilerParams(vmem_limit_bytes=4 * 1024 * 1024)
    line = lambda count: jax.ShapeDtypeStruct((count, LANES), jnp.float32)
    block = lambda f, r: jax.ShapeDtypeStruct((f, r, cols, channels), jnp.bfloat16)
    held = lambda f, r: pltpu.VMEM((f, r, cols, channels), jnp.bfloat16)
    dmas = lambda count: pltpu.SemaphoreType.DMA((count,))
    taps = lambda weight: weight.reshape(9, 3, channels, outputs)
    mixed = pltpu.VMEM((2, 3, 3, channels, outputs), jnp.bfloat16)
    stay = lambda value: pltpu.with_memory_space_constraint(value, pltpu.HBM)
    spread_over = lambda lines, axis: lax.all_to_all(lines, axis, 0, 0, tiled=True)
    vectors = [v.reshape(1, channels) for v in (first_gain, first_shift, second_gain, second_shift)]

    prev = next_frames(features)
    lines, kept, vectors = pl.pallas_call(
        stats_kernel,
        out_shape=[line(band), block(frames, rows), jax.ShapeDtypeStruct((8, channels), jnp.float32)],
        in_specs=[hbm] * 5,
        out_specs=[vmem] * 3,
        scratch_shapes=[dmas(frames + 4)],
        compiler_params=small,
        name="moments",
    )(stay(features), *[stay(v) for v in vectors])
    lines = spread_over(lines, "band")
    lines, pair, cross = pl.pallas_call(
        functools.partial(edges_kernel, members),
        out_shape=[line(tm), block(frames + 2, 2), block(frames + 2, 2)],
        in_specs=[vmem] * 3,
        out_specs=[vmem] * 3,
        compiler_params=small,
        cost_estimate=pl.CostEstimate(flops=4 * 10**9, bytes_accessed=0, transcendentals=0),
        name="edges",
    )(lines, kept, prev)
    pair = swapped(pair, "band", 0)
    cross = swapped(cross, "band", 1)
    lines = spread_over(lines, "tm")

    hidden, lines = pl.pallas_call(
        functools.partial(first_kernel, members),
        out_shape=[block(frames, rows + 2), line(8)],
        in_specs=[vmem] * 7,
        out_specs=[vmem, vmem],
        scratch_shapes=[held(4, rows + 4), mixed],
        compiler_params=params,
        name="first_conv",
    )(kept, prev, pair, cross, lines, vectors, taps(first_weight))

    xz = [[(4 * x + y) * band + b for x in range(4) for b in range(band)] for y in range(4)]
    def rot(v, by):
        return lax.ppermute(v, "tm", [(i, i - i % 4 + (i + by) % 4) for i in range(tm)])
    got = [rot(lines, by) for by in (2, 1, 3)]
    lines = pl.pallas_call(
        functools.partial(ring_merge_kernel, members),
        out_shape=line(64),
        in_specs=[vmem] * 4,
        out_specs=vmem,
        compiler_params=small,
        cost_estimate=pl.CostEstimate(flops=20 * 10**9, bytes_accessed=0, transcendentals=0),
        name="merge",
    )(lines, *got)
    prev = next_frames(hidden)
    lines = lax.all_to_all(lines, ("tm", "band"), 0, 0, tiled=True, axis_index_groups=xz)

    return pl.pallas_call(
        functools.partial(second_kernel, members),
        out_shape=block(frames, rows),
        in_specs=[vmem] * 6,
        out_specs=hbm,
        scratch_shapes=[held(4, rows + 2), mixed, held(frames, rows), dmas(frames)],
        compiler_params=params,
        name="second_conv",
    )(hidden, prev, lines, vectors, kept, taps(second_weight))


def solution(mesh):
    in_specs = (P("tm", "band", None, None), P(), P(), P(), P(), P(), P())
    out_specs = P("tm", "band", None, None)
    return jax.shard_map(local, mesh=mesh, in_specs=in_specs, out_specs=out_specs, check_vma=False)
```

```python
import functools

import jax
import jax.numpy as jnp
from jax import lax
from jax.experimental import pallas as pl
from jax.experimental.pallas import tpu as pltpu
from jax.sharding import PartitionSpec as P

GROUPS = 32
EPSILON = 1e-06
LANES = 128
VMEM_LIMIT = 32 * 1024 * 1024


def next_frames(value):
    count = lax.axis_size("tm")
    return lax.ppermute(value, "tm", [(i, i + 1) for i in range(count - 1)])


def swapped(value, axis, first):
    count = lax.axis_size(axis)
    pairs = []
    for i in range(first, count - 1, 2):
        pairs += [(i, i + 1), (i + 1, i)]
    return lax.ppermute(value, axis, pairs)


def indicator(rows, cols, fn):
    r = lax.broadcasted_iota(jnp.int32, (rows, cols), 0)
    c = lax.broadcasted_iota(jnp.int32, (rows, cols), 1)
    return jnp.where(fn(r, c), 1.0, 0.0).astype(jnp.bfloat16)


def picked(line, pick):
    parts = []
    for _ in range(3):
        parts.append(line.astype(jnp.bfloat16).astype(jnp.float32))
        line = line - parts[-1]
    row = lax.broadcasted_iota(jnp.int32, (16, line.shape[1]), 0)
    stacked = jnp.where(row == 0, parts[0], jnp.where(row == 1, parts[1], jnp.where(row == 2, parts[2], 0.0)))
    product = jnp.dot(stacked.astype(jnp.bfloat16), pick, preferred_element_type=jnp.float32)
    return jnp.sum(product, axis=0, keepdims=True)


def folded(block):
    cols, channels = block.shape
    return jnp.sum(block.reshape(cols // 8, 8, channels), axis=0)


def local_moments(rows, channels):
    size = channels // GROUPS
    same = indicator(channels, channels, lambda r, c: r // size == c // size)
    first = indicator(channels, LANES, lambda r, c: r // size == c)
    second = indicator(channels, LANES, lambda r, c: r // size + GROUPS == c)
    total = folded(rows[0]().astype(jnp.float32))
    for row in rows[1:]:
        total = total + folded(row().astype(jnp.float32))
    positions = len(rows) * rows[0]().shape[0]
    centre = jnp.sum(total, axis=0, keepdims=True) * (1.0 / positions)
    spread = None
    for row in rows:
        off = row().astype(jnp.float32) - centre
        part = folded(off * off)
        spread = part if spread is None else spread + part
    apart = centre - picked(centre, same) * (1.0 / size)
    spread = jnp.sum(spread, axis=0, keepdims=True) + positions * apart * apart
    return picked(centre, first) * (1.0 / size) + picked(spread, second)


def merged_lines(lines, members):
    count = lines.shape[0]
    total = jnp.sum(lines, axis=0, keepdims=True)
    mean = total * (1.0 / count)
    off = lines - mean
    between = jnp.sum(off * off, axis=0, keepdims=True) * members
    lane = lax.broadcasted_iota(jnp.int32, (1, LANES), 1)
    between = jnp.broadcast_to(between, (8, LANES))
    between = pltpu.roll(between, GROUPS, 1)[:1]
    return jnp.where(lane < GROUPS, mean, jnp.where(lane < 2 * GROUPS, total + between, 0.0))


def channel_moments(line, members, channels):
    size = channels // GROUPS
    pick = indicator(LANES, 2 * channels, lambda r, c: c // size == r)
    wide = picked(line, pick)
    centre, variance = wide[:, :channels], wide[:, channels:] * (1.0 / members)
    return centre, lax.rsqrt(variance + EPSILON)


def activated(x, centre, scale, offset):
    half = (x.astype(jnp.float32) - centre) * scale + offset
    return half + half * jnp.tanh(half)


def mixed_frames(act_ref, row, frames):
    first, second, third, fourth = frames
    for part, value in enumerate((first - third, second + third, third - second, second - fourth)):
        act_ref[part, row] = value.astype(jnp.bfloat16)


def mix_weight(weight_ref, mixed_ref):
    for t in range(9):
        first, middle, last = (weight_ref[3 * i + t // 3, t % 3].astype(jnp.float32) for i in range(3))
        ends = 0.5 * (first + last)
        middle = 0.5 * middle
        mixed_ref[0, t // 3, t % 3] = (ends + middle).astype(jnp.bfloat16)
        mixed_ref[1, t // 3, t % 3] = (ends - middle).astype(jnp.bfloat16)


def convolved(act_ref, weight_ref, mixed_ref, pieces):
    cols, channels = act_ref.shape[2:]
    row_count = sum(count for _, count in pieces)
    windows = [
        jnp.concatenate(
            [
                jnp.concatenate(
                    [act_ref[part, first + j : first + j + count].reshape(count * cols, channels) for first, count in pieces]
                )
                for j in range(3)
            ],
            axis=-1,
        )
        for part in range(4)
    ]
    early = late = None
    for k in range(3):
        taps = weight_ref[0:3, k], mixed_ref[0, :, k], mixed_ref[1, :, k], weight_ref[6:9, k]
        first, second, third, fourth = (
            jnp.dot(window, tap.reshape(3 * channels, -1), preferred_element_type=jnp.float32).reshape(row_count, cols, -1)
            for window, tap in zip(windows, taps)
        )
        pair = first + second + third, second - third - fourth
        if k != 1:
            column = lax.broadcasted_iota(jnp.int32, first.shape, 1)
            edge, by = (0, 1) if k == 0 else (cols - 1, cols - 1)
            pair = [jnp.where(column == edge, value, pltpu.roll(value, by, 1)) for value in pair]
        early = pair[0] if early is None else early + pair[0]
        late = pair[1] if late is None else late + pair[1]
    return early, late


def places(rows):
    even = lax.rem(lax.axis_index("band"), 2) == 0
    pair_at, cross_at = jnp.where(even, rows + 2, 0), jnp.where(even, 0, rows + 2)
    pair_from, cross_from = jnp.where(even, rows - 2, 0), jnp.where(even, 0, rows - 2)
    return pair_at, cross_at, pair_from, cross_from


def stats_kernel(x_ref, *refs):
    vectors, (line_ref, kept_ref, params_ref, sems) = refs[:4], refs[4:]
    frames, rows, _, channels = x_ref.shape
    copies = [pltpu.make_async_copy(x_ref.at[f], kept_ref.at[f], sems.at[f]) for f in range(frames)]
    copies += [
        pltpu.make_async_copy(vector, params_ref.at[pl.ds(i, 1)], sems.at[frames + i])
        for i, vector in enumerate(vectors)
    ]
    for copy in copies:
        copy.start()
    for copy in copies:
        copy.wait()
    reads = [functools.partial(lambda f, r: kept_ref[f, r], f, r) for f in range(frames) for r in range(rows)]
    line_ref[...] = jnp.broadcast_to(local_moments(reads, channels), line_ref.shape)


def edges_kernel(x_ref, prev_ref, after_ref, cross_ref, pair_ref):
    _, _, pair_from, cross_from = places(x_ref.shape[1])
    for out_ref, at in ((pair_ref, pair_from), (cross_ref, cross_from)):
        out_ref[0:2] = prev_ref[:, pl.ds(at, 2)]
        out_ref[2:4] = x_ref[:, pl.ds(at, 2)]


def ring_merge_kernel(members, a_ref, b_ref, c_ref, d_ref, *refs):
    lines = jnp.concatenate([r[0:1] for r in (a_ref, b_ref, c_ref, d_ref)], axis=0)
    refs[-1][...] = jnp.broadcast_to(merged_lines(lines, members), refs[-1].shape)


def merge_kernel(members, lines_ref, line_ref):
    line_ref[...] = jnp.broadcast_to(merged_lines(lines_ref[...], members), line_ref.shape)


def scaling(lines_ref, params_ref, norm, members):
    channels = params_ref.shape[1]
    devices = lax.axis_size("tm") * lax.axis_size("band")
    line = merged_lines(lines_ref[...], members * devices // lines_ref.shape[0]) if norm else lines_ref[0:1]
    centre, inverse = channel_moments(line, members * devices, channels)
    gain, shift = params_ref[2 * norm : 2 * norm + 1], params_ref[2 * norm + 1 : 2 * norm + 2]
    return centre, 0.5 * inverse * gain, 0.5 * shift


def at_ends():
    band = lax.axis_index("band")
    return lax.axis_index("tm") == 0, band == 0, band == lax.axis_size("band") - 1


def first_rows(act_ref, out_ref, weight_ref, mixed_ref, pieces):
    for f, value in enumerate(convolved(act_ref, weight_ref, mixed_ref, pieces)):
        done = 0
        for first, count in pieces:
            out_ref[f, first : first + count] = value[done : done + count].astype(jnp.bfloat16)
            done += count


def inner_kernel(members, x_ref, prev_ref, lines_ref, params_ref, weight_ref, hidden_ref, act_ref, mixed_ref):
    rows = x_ref.shape[1]
    leading, _, _ = at_ends()
    norm = scaling(lines_ref, params_ref, 0, members)
    for r in range(rows):
        own = [x_ref[f, r] for f in range(2)]
        before = [jnp.where(leading, own[0], prev_ref[f, r]) for f in range(2)]
        mixed_frames(act_ref, r + 2, [activated(x, *norm) for x in before + own])
    mix_weight(weight_ref, mixed_ref)
    first_rows(act_ref, hidden_ref, weight_ref, mixed_ref, [(2, rows - 2)])


def outer_kernel(members, x_ref, prev_ref, cross_ref, pair_ref, lines_ref, params_ref, weight_ref, mixed_ref, _, __,
                 hidden_ref, act_ref, line_ref):
    frames, rows, _, channels = x_ref.shape
    leading, top, bottom = at_ends()
    even = lax.rem(lax.axis_index("band"), 2) == 0
    norm = scaling(lines_ref, params_ref, 0, members)

    def row_of(f, r):
        inner = prev_ref if f < 2 else x_ref
        if r < 2:
            outer = jnp.where(even, cross_ref[f, r], pair_ref[f, r])
            return jnp.where(top, inner[f % 2, 0], outer) if r == 1 else outer
        outer = jnp.where(even, pair_ref[f, r - rows - 2], cross_ref[f, r - rows - 2])
        return jnp.where(bottom, inner[f % 2, rows - 1], outer) if r == rows + 2 else outer

    for r in (0, 1, rows + 2, rows + 3):
        own = [row_of(f, r) for f in (2, 3)]
        before = [jnp.where(leading, own[0], row_of(f, r)) for f in (0, 1)]
        mixed_frames(act_ref, r, [activated(x, *norm) for x in before + own])
    first_rows(act_ref, hidden_ref, weight_ref, mixed_ref, [(0, 2), (rows, 2)])
    reads = [functools.partial(lambda f, r: hidden_ref[f, r + 1], f, r) for f in range(frames) for r in range(rows)]
    line_ref[...] = jnp.broadcast_to(local_moments(reads, channels), line_ref.shape)


def second_kernel(members, hidden_ref, prev_ref, lines_ref, params_ref, x_ref, weight_ref, out_ref,
                  act_ref, mixed_ref, made_ref, out_sems):
    frames, rows, cols, channels = x_ref.shape
    leading, top, bottom = at_ends()
    norm = scaling(lines_ref, params_ref, 1, members)

    def row_of(f, r):
        ref = prev_ref if f < 2 else hidden_ref
        if r == 0:
            return jnp.where(top, ref[f % 2, 1], ref[f % 2, 0])
        if r == rows + 1:
            return jnp.where(bottom, ref[f % 2, rows], ref[f % 2, rows + 1])
        return ref[f % 2, r]

    for r in range(rows + 2):
        own = [row_of(f, r) for f in (2, 3)]
        before = [jnp.where(leading, own[0], row_of(f, r)) for f in (0, 1)]
        mixed_frames(act_ref, r, [activated(x, *norm) for x in before + own])
    mix_weight(weight_ref, mixed_ref)
    outs = []
    for f, value in enumerate(convolved(act_ref, weight_ref, mixed_ref, [(0, rows)])):
        made_ref[f] = (x_ref[f].astype(jnp.float32) + value).astype(jnp.bfloat16)
        outs.append(pltpu.make_async_copy(made_ref.at[f], out_ref.at[f], out_sems.at[f]))
        outs[-1].start()
    for copy in outs:
        copy.wait()


def local(
    features, first_gain, first_shift, first_weight, second_gain, second_shift, second_weight
):
    frames, rows, cols, channels = features.shape
    outputs = first_weight.shape[-1]
    tm, band = lax.axis_size("tm"), lax.axis_size("band")
    members = frames * rows * cols * (channels // GROUPS)
    vmem = pl.BlockSpec(memory_space=pltpu.VMEM)
    hbm = pl.BlockSpec(memory_space=pltpu.HBM)
    anywhere = pl.BlockSpec(memory_space=pl.ANY)
    params = pltpu.CompilerParams(vmem_limit_bytes=VMEM_LIMIT)
    small = pltpu.CompilerParams(vmem_limit_bytes=4 * 1024 * 1024)
    line = lambda count: jax.ShapeDtypeStruct((count, LANES), jnp.float32)
    block = lambda f, r: jax.ShapeDtypeStruct((f, r, cols, channels), jnp.bfloat16)
    held = lambda f, r: pltpu.VMEM((f, r, cols, channels), jnp.bfloat16)
    dmas = lambda count: pltpu.SemaphoreType.DMA((count,))
    taps = lambda weight: weight.reshape(9, 3, channels, outputs)
    mixed = pltpu.VMEM((2, 3, 3, channels, outputs), jnp.bfloat16)
    stay = lambda value: pltpu.with_memory_space_constraint(value, pltpu.HBM)
    vectors = [v.reshape(1, channels) for v in (first_gain, first_shift, second_gain, second_shift)]

    prev = next_frames(features)
    lines, kept, vectors = pl.pallas_call(
        stats_kernel,
        out_shape=[line(64), block(frames, rows), jax.ShapeDtypeStruct((8, channels), jnp.float32)],
        in_specs=[hbm] * 5,
        out_specs=[vmem] * 3,
        scratch_shapes=[dmas(frames + 4)],
        compiler_params=small,
        name="moments",
    )(stay(features), *[stay(v) for v in vectors])
    others = [[(4 * x + y) * band + b for x in range(4) for b in range(band)] for y in range(4)]
    over_others = lambda lines: lax.all_to_all(lines, ("tm", "band"), 0, 0, tiled=True, axis_index_groups=others)
    around = lambda line, by: lax.ppermute(line, "tm", [(i, i - i % 4 + (i + by) % 4) for i in range(tm)])

    def over_y(lines, members, count, *ready):
        return pl.pallas_call(
            functools.partial(ring_merge_kernel, members),
            out_shape=line(count),
            in_specs=[vmem] * (4 + len(ready)),
            out_specs=vmem,
            compiler_params=small,
            cost_estimate=pl.CostEstimate(flops=20 * 10**9, bytes_accessed=0, transcendentals=0),
            name="merge_y",
        )(lines, *[around(lines, by) for by in (2, 1, 3)], *ready)

    lines = pl.pallas_call(
        functools.partial(merge_kernel, members),
        out_shape=line(8),
        in_specs=[vmem],
        out_specs=vmem,
        compiler_params=small,
        name="merge",
    )(over_others(lines))
    cross, pair = pl.pallas_call(
        edges_kernel,
        out_shape=[block(frames + 2, 2), block(frames + 2, 2)],
        in_specs=[vmem] * 3,
        out_specs=[vmem] * 2,
        compiler_params=small,
        cost_estimate=pl.CostEstimate(flops=4 * 10**9, bytes_accessed=0, transcendentals=0),
        name="edges",
    )(kept, prev, lines)
    cross = swapped(cross, "band", 1)
    pair = swapped(pair, "band", 0)
    first_weight = taps(first_weight)
    lines = over_y(lines, 64 * members, 8, first_weight)

    hidden, act, mixed_weight = pl.pallas_call(
        functools.partial(inner_kernel, members),
        out_shape=[
            block(frames, rows + 2),
            block(4, rows + 4),
            jax.ShapeDtypeStruct((2, 3, 3, channels, outputs), jnp.bfloat16),
        ],
        in_specs=[vmem] * 5,
        out_specs=[vmem] * 3,
        compiler_params=params,
        name="first_conv_inner",
    )(kept, prev, lines, vectors, first_weight)
    hidden, _, lines = pl.pallas_call(
        functools.partial(outer_kernel, members),
        out_shape=[block(frames, rows + 2), block(4, rows + 4), line(8)],
        in_specs=[vmem] * 10,
        out_specs=[vmem] * 3,
        input_output_aliases={8: 0, 9: 1},
        compiler_params=params,
        name="first_conv_outer",
    )(kept, prev, cross, pair, lines, vectors, first_weight, mixed_weight, hidden, act)

    prev = next_frames(hidden)
    lines = over_others(over_y(lines, members, 64))

    return pl.pallas_call(
        functools.partial(second_kernel, members),
        out_shape=block(frames, rows),
        in_specs=[vmem] * 6,
        out_specs=hbm,
        scratch_shapes=[held(4, rows + 2), mixed, held(frames, rows), dmas(frames)],
        compiler_params=params,
        name="second_conv",
    )(hidden, prev, lines, vectors, kept, taps(second_weight))


def solution(mesh):
    in_specs = (P("tm", "band", None, None), P(), P(), P(), P(), P(), P())
    out_specs = P("tm", "band", None, None)
    return jax.shard_map(local, mesh=mesh, in_specs=in_specs, out_specs=out_specs, check_vma=False)
```

```python
import functools

import jax
import jax.numpy as jnp
from jax import lax
from jax.experimental import pallas as pl
from jax.experimental.pallas import tpu as pltpu
from jax.sharding import PartitionSpec as P

GROUPS = 32
EPSILON = 1e-06
LANES = 128
VMEM_LIMIT = 32 * 1024 * 1024


def next_frames(value):
    count = lax.axis_size("tm")
    return lax.ppermute(value, "tm", [(i, i + 1) for i in range(count - 1)])


def swapped(value, axis, first):
    count = lax.axis_size(axis)
    pairs = []
    for i in range(first, count - 1, 2):
        pairs += [(i, i + 1), (i + 1, i)]
    return lax.ppermute(value, axis, pairs)


def indicator(rows, cols, fn):
    r = lax.broadcasted_iota(jnp.int32, (rows, cols), 0)
    c = lax.broadcasted_iota(jnp.int32, (rows, cols), 1)
    return jnp.where(fn(r, c), 1.0, 0.0).astype(jnp.bfloat16)


def picked(line, pick):
    parts = []
    for _ in range(3):
        parts.append(line.astype(jnp.bfloat16).astype(jnp.float32))
        line = line - parts[-1]
    row = lax.broadcasted_iota(jnp.int32, (16, line.shape[1]), 0)
    stacked = jnp.where(row == 0, parts[0], jnp.where(row == 1, parts[1], jnp.where(row == 2, parts[2], 0.0)))
    product = jnp.dot(stacked.astype(jnp.bfloat16), pick, preferred_element_type=jnp.float32)
    return jnp.sum(product, axis=0, keepdims=True)


def folded(block):
    cols, channels = block.shape
    return jnp.sum(block.reshape(cols // 8, 8, channels), axis=0)


def local_moments(rows, channels):
    size = channels // GROUPS
    same = indicator(channels, channels, lambda r, c: r // size == c // size)
    first = indicator(channels, LANES, lambda r, c: r // size == c)
    second = indicator(channels, LANES, lambda r, c: r // size + GROUPS == c)
    total = folded(rows[0]().astype(jnp.float32))
    for row in rows[1:]:
        total = total + folded(row().astype(jnp.float32))
    positions = len(rows) * rows[0]().shape[0]
    centre = jnp.sum(total, axis=0, keepdims=True) * (1.0 / positions)
    spread = None
    for row in rows:
        off = row().astype(jnp.float32) - centre
        part = folded(off * off)
        spread = part if spread is None else spread + part
    apart = centre - picked(centre, same) * (1.0 / size)
    spread = jnp.sum(spread, axis=0, keepdims=True) + positions * apart * apart
    return picked(centre, first) * (1.0 / size) + picked(spread, second)


def merged_lines(lines, members):
    count = lines.shape[0]
    total = jnp.sum(lines, axis=0, keepdims=True)
    mean = total * (1.0 / count)
    off = lines - mean
    between = jnp.sum(off * off, axis=0, keepdims=True) * members
    lane = lax.broadcasted_iota(jnp.int32, (1, LANES), 1)
    between = jnp.broadcast_to(between, (8, LANES))
    between = pltpu.roll(between, GROUPS, 1)[:1]
    return jnp.where(lane < GROUPS, mean, jnp.where(lane < 2 * GROUPS, total + between, 0.0))


def channel_moments(line, members, channels):
    size = channels // GROUPS
    pick = indicator(LANES, 2 * channels, lambda r, c: c // size == r)
    wide = picked(line, pick)
    centre, variance = wide[:, :channels], wide[:, channels:] * (1.0 / members)
    return centre, lax.rsqrt(variance + EPSILON)


def activated(x, centre, scale, offset):
    half = (x.astype(jnp.float32) - centre) * scale + offset
    return half + half * jnp.tanh(half)


def mixed_frames(act_ref, row, frames):
    first, second, third, fourth = frames
    for part, value in enumerate((first - third, second + third, third - second, second - fourth)):
        act_ref[part, row] = value.astype(jnp.bfloat16)


def mix_weight(weight_ref, mixed_ref):
    for t in range(9):
        first, middle, last = (weight_ref[3 * i + t // 3, t % 3].astype(jnp.float32) for i in range(3))
        ends = 0.5 * (first + last)
        middle = 0.5 * middle
        mixed_ref[0, t // 3, t % 3] = (ends + middle).astype(jnp.bfloat16)
        mixed_ref[1, t // 3, t % 3] = (ends - middle).astype(jnp.bfloat16)


def convolved(act_ref, weight_ref, mixed_ref, pieces):
    cols, channels = act_ref.shape[2:]
    row_count = sum(count for _, count in pieces)
    windows = [
        jnp.concatenate(
            [
                jnp.concatenate(
                    [act_ref[part, pl.ds(first + j, count)].reshape(count * cols, channels) for first, count in pieces]
                )
                for j in range(3)
            ],
            axis=-1,
        )
        for part in range(4)
    ]
    early = late = None
    for k in range(3):
        taps = weight_ref[0:3, k], mixed_ref[0, :, k], mixed_ref[1, :, k], weight_ref[6:9, k]
        first, second, third, fourth = (
            jnp.dot(window, tap.reshape(3 * channels, -1), preferred_element_type=jnp.float32).reshape(row_count, cols, -1)
            for window, tap in zip(windows, taps)
        )
        pair = first + second + third, second - third - fourth
        if k != 1:
            column = lax.broadcasted_iota(jnp.int32, first.shape, 1)
            edge, by = (0, 1) if k == 0 else (cols - 1, cols - 1)
            pair = [jnp.where(column == edge, value, pltpu.roll(value, by, 1)) for value in pair]
        early = pair[0] if early is None else early + pair[0]
        late = pair[1] if late is None else late + pair[1]
    return early, late


def places(rows):
    even = lax.rem(lax.axis_index("band"), 2) == 0
    pair_at, cross_at = jnp.where(even, rows + 2, 0), jnp.where(even, 0, rows + 2)
    pair_from, cross_from = jnp.where(even, rows - 2, 0), jnp.where(even, 0, rows - 2)
    return pair_at, cross_at, pair_from, cross_from


def stats_kernel(x_ref, *refs):
    vectors, (line_ref, kept_ref, params_ref, sems) = refs[:4], refs[4:]
    frames, rows, _, channels = x_ref.shape
    copies = [pltpu.make_async_copy(x_ref.at[f], kept_ref.at[f], sems.at[f]) for f in range(frames)]
    copies += [
        pltpu.make_async_copy(vector, params_ref.at[pl.ds(i, 1)], sems.at[frames + i])
        for i, vector in enumerate(vectors)
    ]
    for copy in copies:
        copy.start()
    for copy in copies:
        copy.wait()
    reads = [functools.partial(lambda f, r: kept_ref[f, r], f, r) for f in range(frames) for r in range(rows)]
    line_ref[...] = jnp.broadcast_to(local_moments(reads, channels), line_ref.shape)


def edges_kernel(x_ref, prev_ref, after_ref, cross_ref, pair_ref):
    _, _, pair_from, cross_from = places(x_ref.shape[1])
    for out_ref, at in ((pair_ref, pair_from), (cross_ref, cross_from)):
        out_ref[0:2] = prev_ref[:, pl.ds(at, 2)]
        out_ref[2:4] = x_ref[:, pl.ds(at, 2)]


def ring_merge_kernel(members, a_ref, b_ref, c_ref, d_ref, *refs):
    lines = jnp.concatenate([r[0:1] for r in (a_ref, b_ref, c_ref, d_ref)], axis=0)
    refs[-1][...] = jnp.broadcast_to(merged_lines(lines, members), refs[-1].shape)


def merge_kernel(members, lines_ref, line_ref):
    line_ref[...] = jnp.broadcast_to(merged_lines(lines_ref[...], members), line_ref.shape)


def scaling(lines_ref, params_ref, norm, members):
    channels = params_ref.shape[1]
    devices = lax.axis_size("tm") * lax.axis_size("band")
    line = merged_lines(lines_ref[...], members * devices // lines_ref.shape[0]) if norm else lines_ref[0:1]
    centre, inverse = channel_moments(line, members * devices, channels)
    gain, shift = params_ref[2 * norm : 2 * norm + 1], params_ref[2 * norm + 1 : 2 * norm + 2]
    return centre, 0.5 * inverse * gain, 0.5 * shift


def at_ends():
    band = lax.axis_index("band")
    return lax.axis_index("tm") == 0, band == 0, band == lax.axis_size("band") - 1


def first_rows(act_ref, out_ref, weight_ref, mixed_ref, pieces):
    for f, value in enumerate(convolved(act_ref, weight_ref, mixed_ref, pieces)):
        done = 0
        for first, count in pieces:
            out_ref[f, pl.ds(first, count)] = value[done : done + count].astype(jnp.bfloat16)
            done += count


def inner_kernel(members, x_ref, prev_ref, pair_ref, lines_ref, params_ref, weight_ref, hidden_ref, act_ref, mixed_ref):
    rows = x_ref.shape[1]
    leading, _, _ = at_ends()
    pair_at, _, _, _ = places(rows)
    norm = scaling(lines_ref, params_ref, 0, members)

    def row(at, before, own):
        before = [jnp.where(leading, own[0], x) for x in before]
        mixed_frames(act_ref, at, [activated(x, *norm) for x in before + own])

    for r in range(rows):
        row(r + 2, [prev_ref[f, r] for f in range(2)], [x_ref[f, r] for f in range(2)])
    for r in range(2):
        row(pair_at + r, [pair_ref[f, r] for f in (0, 1)], [pair_ref[f, r] for f in (2, 3)])
    mix_weight(weight_ref, mixed_ref)
    first_rows(act_ref, hidden_ref, weight_ref, mixed_ref, [(2, rows - 2), (jnp.minimum(pair_at, rows), 2)])


def outer_kernel(members, x_ref, prev_ref, cross_ref, lines_ref, params_ref, weight_ref, mixed_ref, _, __,
                 hidden_ref, act_ref, line_ref):
    frames, rows, _, channels = x_ref.shape
    leading, top, bottom = at_ends()
    _, cross_at, _, _ = places(rows)
    norm = scaling(lines_ref, params_ref, 0, members)
    for r in range(2):
        rim = [jnp.where(top, ref[f, 0], ref[f, rows - 1]) for ref in (prev_ref, x_ref) for f in range(2)]
        values = [jnp.where(top | bottom, rim[f], cross_ref[f, r]) for f in range(4)]
        before = [jnp.where(leading, values[2], x) for x in values[:2]]
        mixed_frames(act_ref, cross_at + r, [activated(x, *norm) for x in before + values[2:]])
    first_rows(act_ref, hidden_ref, weight_ref, mixed_ref, [(jnp.minimum(cross_at, rows), 2)])
    reads = [functools.partial(lambda f, r: hidden_ref[f, r + 1], f, r) for f in range(frames) for r in range(rows)]
    line_ref[...] = jnp.broadcast_to(local_moments(reads, channels), line_ref.shape)


def second_kernel(members, hidden_ref, prev_ref, lines_ref, params_ref, x_ref, weight_ref, out_ref,
                  act_ref, mixed_ref, made_ref, out_sems):
    frames, rows, cols, channels = x_ref.shape
    leading, top, bottom = at_ends()
    norm = scaling(lines_ref, params_ref, 1, members)

    def row_of(f, r):
        ref = prev_ref if f < 2 else hidden_ref
        if r == 0:
            return jnp.where(top, ref[f % 2, 1], ref[f % 2, 0])
        if r == rows + 1:
            return jnp.where(bottom, ref[f % 2, rows], ref[f % 2, rows + 1])
        return ref[f % 2, r]

    for r in range(rows + 2):
        own = [row_of(f, r) for f in (2, 3)]
        before = [jnp.where(leading, own[0], row_of(f, r)) for f in (0, 1)]
        mixed_frames(act_ref, r, [activated(x, *norm) for x in before + own])
    mix_weight(weight_ref, mixed_ref)
    outs = []
    for f, value in enumerate(convolved(act_ref, weight_ref, mixed_ref, [(0, rows)])):
        made_ref[f] = (x_ref[f].astype(jnp.float32) + value).astype(jnp.bfloat16)
        outs.append(pltpu.make_async_copy(made_ref.at[f], out_ref.at[f], out_sems.at[f]))
        outs[-1].start()
    for copy in outs:
        copy.wait()


def local(
    features, first_gain, first_shift, first_weight, second_gain, second_shift, second_weight
):
    frames, rows, cols, channels = features.shape
    outputs = first_weight.shape[-1]
    tm, band = lax.axis_size("tm"), lax.axis_size("band")
    members = frames * rows * cols * (channels // GROUPS)
    vmem = pl.BlockSpec(memory_space=pltpu.VMEM)
    hbm = pl.BlockSpec(memory_space=pltpu.HBM)
    anywhere = pl.BlockSpec(memory_space=pl.ANY)
    params = pltpu.CompilerParams(vmem_limit_bytes=VMEM_LIMIT)
    small = pltpu.CompilerParams(vmem_limit_bytes=4 * 1024 * 1024)
    line = lambda count: jax.ShapeDtypeStruct((count, LANES), jnp.float32)
    block = lambda f, r: jax.ShapeDtypeStruct((f, r, cols, channels), jnp.bfloat16)
    held = lambda f, r: pltpu.VMEM((f, r, cols, channels), jnp.bfloat16)
    dmas = lambda count: pltpu.SemaphoreType.DMA((count,))
    taps = lambda weight: weight.reshape(9, 3, channels, outputs)
    mixed = pltpu.VMEM((2, 3, 3, channels, outputs), jnp.bfloat16)
    stay = lambda value: pltpu.with_memory_space_constraint(value, pltpu.HBM)
    vectors = [v.reshape(1, channels) for v in (first_gain, first_shift, second_gain, second_shift)]

    prev = next_frames(features)
    lines, kept, vectors = pl.pallas_call(
        stats_kernel,
        out_shape=[line(64), block(frames, rows), jax.ShapeDtypeStruct((8, channels), jnp.float32)],
        in_specs=[hbm] * 5,
        out_specs=[vmem] * 3,
        scratch_shapes=[dmas(frames + 4)],
        compiler_params=small,
        name="moments",
    )(stay(features), *[stay(v) for v in vectors])
    others = [[(4 * x + y) * band + b for x in range(4) for b in range(band)] for y in range(4)]
    over_others = lambda lines: lax.all_to_all(lines, ("tm", "band"), 0, 0, tiled=True, axis_index_groups=others)
    around = lambda line, by: lax.ppermute(line, "tm", [(i, i - i % 4 + (i + by) % 4) for i in range(tm)])

    def over_y(lines, members, count, *ready):
        return pl.pallas_call(
            functools.partial(ring_merge_kernel, members),
            out_shape=line(count),
            in_specs=[vmem] * (4 + len(ready)),
            out_specs=vmem,
            compiler_params=small,
            cost_estimate=pl.CostEstimate(flops=20 * 10**9, bytes_accessed=0, transcendentals=0),
            name="merge_y",
        )(lines, *[around(lines, by) for by in (2, 1, 3)], *ready)

    lines = pl.pallas_call(
        functools.partial(merge_kernel, members),
        out_shape=line(8),
        in_specs=[vmem],
        out_specs=vmem,
        compiler_params=small,
        name="merge",
    )(over_others(lines))
    cross, pair = pl.pallas_call(
        edges_kernel,
        out_shape=[block(frames + 2, 2), block(frames + 2, 2)],
        in_specs=[vmem] * 3,
        out_specs=[vmem] * 2,
        compiler_params=small,
        cost_estimate=pl.CostEstimate(flops=4 * 10**9, bytes_accessed=0, transcendentals=0),
        name="edges",
    )(kept, prev, lines)
    cross = swapped(cross, "band", 1)
    pair = swapped(pair, "band", 0)
    first_weight = taps(first_weight)
    lines = over_y(lines, 64 * members, 8, first_weight, pair)

    hidden, act, mixed_weight = pl.pallas_call(
        functools.partial(inner_kernel, members),
        out_shape=[
            block(frames, rows + 2),
            block(4, rows + 4),
            jax.ShapeDtypeStruct((2, 3, 3, channels, outputs), jnp.bfloat16),
        ],
        in_specs=[vmem] * 6,
        out_specs=[vmem] * 3,
        compiler_params=params,
        name="first_conv_inner",
    )(kept, prev, pair, lines, vectors, first_weight)
    hidden, _, lines = pl.pallas_call(
        functools.partial(outer_kernel, members),
        out_shape=[block(frames, rows + 2), block(4, rows + 4), line(8)],
        in_specs=[vmem] * 9,
        out_specs=[vmem] * 3,
        input_output_aliases={7: 0, 8: 1},
        compiler_params=params,
        name="first_conv_outer",
    )(kept, prev, cross, lines, vectors, first_weight, mixed_weight, hidden, act)

    prev = next_frames(hidden)
    lines = over_others(over_y(lines, members, 64))

    return pl.pallas_call(
        functools.partial(second_kernel, members),
        out_shape=block(frames, rows),
        in_specs=[vmem] * 6,
        out_specs=hbm,
        scratch_shapes=[held(4, rows + 2), mixed, held(frames, rows), dmas(frames)],
        compiler_params=params,
        name="second_conv",
    )(hidden, prev, lines, vectors, kept, taps(second_weight))


def solution(mesh):
    in_specs = (P("tm", "band", None, None), P(), P(), P(), P(), P(), P())
    out_specs = P("tm", "band", None, None)
    return jax.shard_map(local, mesh=mesh, in_specs=in_specs, out_specs=out_specs, check_vma=False)
```

```python
import functools

import jax
import jax.numpy as jnp
from jax import lax
from jax.experimental import pallas as pl
from jax.experimental.pallas import tpu as pltpu
from jax.sharding import PartitionSpec as P

GROUPS = 32
EPSILON = 1e-06
LANES = 128
VMEM_LIMIT = 32 * 1024 * 1024


def next_frames(value):
    count = lax.axis_size("tm")
    return lax.ppermute(value, "tm", [(i, i + 1) for i in range(count - 1)])


def swapped(value, axis, first):
    count = lax.axis_size(axis)
    pairs = []
    for i in range(first, count - 1, 2):
        pairs += [(i, i + 1), (i + 1, i)]
    return lax.ppermute(value, axis, pairs)


def indicator(rows, cols, fn):
    r = lax.broadcasted_iota(jnp.int32, (rows, cols), 0)
    c = lax.broadcasted_iota(jnp.int32, (rows, cols), 1)
    return jnp.where(fn(r, c), 1.0, 0.0).astype(jnp.bfloat16)


def picked(line, pick):
    parts = []
    for _ in range(3):
        parts.append(line.astype(jnp.bfloat16).astype(jnp.float32))
        line = line - parts[-1]
    row = lax.broadcasted_iota(jnp.int32, (16, line.shape[1]), 0)
    stacked = jnp.where(row == 0, parts[0], jnp.where(row == 1, parts[1], jnp.where(row == 2, parts[2], 0.0)))
    product = jnp.dot(stacked.astype(jnp.bfloat16), pick, preferred_element_type=jnp.float32)
    return jnp.sum(product, axis=0, keepdims=True)


def folded(block):
    cols, channels = block.shape
    return jnp.sum(block.reshape(cols // 8, 8, channels), axis=0)


def local_moments(rows, channels):
    size = channels // GROUPS
    same = indicator(channels, channels, lambda r, c: r // size == c // size)
    first = indicator(channels, LANES, lambda r, c: r // size == c)
    second = indicator(channels, LANES, lambda r, c: r // size + GROUPS == c)
    total = folded(rows[0]().astype(jnp.float32))
    for row in rows[1:]:
        total = total + folded(row().astype(jnp.float32))
    positions = len(rows) * rows[0]().shape[0]
    centre = jnp.sum(total, axis=0, keepdims=True) * (1.0 / positions)
    spread = None
    for row in rows:
        off = row().astype(jnp.float32) - centre
        part = folded(off * off)
        spread = part if spread is None else spread + part
    apart = centre - picked(centre, same) * (1.0 / size)
    spread = jnp.sum(spread, axis=0, keepdims=True) + positions * apart * apart
    return picked(centre, first) * (1.0 / size) + picked(spread, second)


def merged_lines(lines, members):
    count = lines.shape[0]
    total = jnp.sum(lines, axis=0, keepdims=True)
    mean = total * (1.0 / count)
    off = lines - mean
    between = jnp.sum(off * off, axis=0, keepdims=True) * members
    lane = lax.broadcasted_iota(jnp.int32, (1, LANES), 1)
    between = jnp.broadcast_to(between, (8, LANES))
    between = pltpu.roll(between, GROUPS, 1)[:1]
    return jnp.where(lane < GROUPS, mean, jnp.where(lane < 2 * GROUPS, total + between, 0.0))


def channel_moments(line, members, channels):
    size = channels // GROUPS
    pick = indicator(LANES, 2 * channels, lambda r, c: c // size == r)
    wide = picked(line, pick)
    centre, variance = wide[:, :channels], wide[:, channels:] * (1.0 / members)
    return centre, lax.rsqrt(variance + EPSILON)


def activated(x, centre, scale, offset):
    half = (x.astype(jnp.float32) - centre) * scale + offset
    return half + half * jnp.tanh(half)


def mixed_frames(act_ref, row, frames):
    first, second, third, fourth = frames
    for part, value in enumerate((first - third, second + third, third - second, second - fourth)):
        act_ref[part, row] = value.astype(jnp.bfloat16)


def mix_weight(weight_ref, mixed_ref):
    for t in range(9):
        first, middle, last = (weight_ref[3 * i + t // 3, t % 3].astype(jnp.float32) for i in range(3))
        ends = 0.5 * (first + last)
        middle = 0.5 * middle
        mixed_ref[0, t // 3, t % 3] = (ends + middle).astype(jnp.bfloat16)
        mixed_ref[1, t // 3, t % 3] = (ends - middle).astype(jnp.bfloat16)


def convolved(act_ref, weight_ref, mixed_ref, pieces):
    cols, channels = act_ref.shape[2:]
    row_count = sum(count for _, count in pieces)
    windows = [
        jnp.concatenate(
            [
                jnp.concatenate(
                    [act_ref[part, pl.ds(first + j, count)].reshape(count * cols, channels) for first, count in pieces]
                )
                for j in range(3)
            ],
            axis=-1,
        )
        for part in range(4)
    ]
    early = late = None
    for k in range(3):
        taps = weight_ref[0:3, k], mixed_ref[0, :, k], mixed_ref[1, :, k], weight_ref[6:9, k]
        first, second, third, fourth = (
            jnp.dot(window, tap.reshape(3 * channels, -1), preferred_element_type=jnp.float32).reshape(row_count, cols, -1)
            for window, tap in zip(windows, taps)
        )
        pair = first + second + third, second - third - fourth
        if k != 1:
            column = lax.broadcasted_iota(jnp.int32, first.shape, 1)
            edge, by = (0, 1) if k == 0 else (cols - 1, cols - 1)
            pair = [jnp.where(column == edge, value, pltpu.roll(value, by, 1)) for value in pair]
        early = pair[0] if early is None else early + pair[0]
        late = pair[1] if late is None else late + pair[1]
    return early, late


def places(rows):
    even = lax.rem(lax.axis_index("band"), 2) == 0
    pair_at, cross_at = jnp.where(even, rows + 2, 0), jnp.where(even, 0, rows + 2)
    pair_from, cross_from = jnp.where(even, rows - 2, 0), jnp.where(even, 0, rows - 2)
    return pair_at, cross_at, pair_from, cross_from


def stats_kernel(x_ref, *refs):
    vectors, (line_ref, kept_ref, params_ref, sems) = refs[:4], refs[4:]
    frames, rows, _, channels = x_ref.shape
    copies = [pltpu.make_async_copy(x_ref.at[f], kept_ref.at[f], sems.at[f]) for f in range(frames)]
    copies += [
        pltpu.make_async_copy(vector, params_ref.at[pl.ds(i, 1)], sems.at[frames + i])
        for i, vector in enumerate(vectors)
    ]
    for copy in copies:
        copy.start()
    for copy in copies:
        copy.wait()
    reads = [functools.partial(lambda f, r: kept_ref[f, r], f, r) for f in range(frames) for r in range(rows)]
    line_ref[...] = jnp.broadcast_to(local_moments(reads, channels), line_ref.shape)


def edges_kernel(x_ref, prev_ref, after_ref, cross_ref, pair_ref):
    _, _, pair_from, cross_from = places(x_ref.shape[1])
    for out_ref, at in ((pair_ref, pair_from), (cross_ref, cross_from)):
        out_ref[0:2] = prev_ref[:, pl.ds(at, 2)]
        out_ref[2:4] = x_ref[:, pl.ds(at, 2)]


def ring_merge_kernel(members, a_ref, b_ref, c_ref, d_ref, *refs):
    lines = jnp.concatenate([r[0:1] for r in (a_ref, b_ref, c_ref, d_ref)], axis=0)
    refs[-1][...] = jnp.broadcast_to(merged_lines(lines, members), refs[-1].shape)


def merge_kernel(members, lines_ref, line_ref):
    line_ref[...] = jnp.broadcast_to(merged_lines(lines_ref[...], members), line_ref.shape)


def scaling(lines_ref, params_ref, norm, members):
    channels = params_ref.shape[1]
    devices = lax.axis_size("tm") * lax.axis_size("band")
    line = merged_lines(lines_ref[...], members * devices // lines_ref.shape[0]) if norm else lines_ref[0:1]
    centre, inverse = channel_moments(line, members * devices, channels)
    gain, shift = params_ref[2 * norm : 2 * norm + 1], params_ref[2 * norm + 1 : 2 * norm + 2]
    return centre, 0.5 * inverse * gain, 0.5 * shift


def at_ends():
    band = lax.axis_index("band")
    return lax.axis_index("tm") == 0, band == 0, band == lax.axis_size("band") - 1


def first_rows(act_ref, out_ref, weight_ref, mixed_ref, pieces):
    for f, value in enumerate(convolved(act_ref, weight_ref, mixed_ref, pieces)):
        done = 0
        for first, count in pieces:
            out_ref[f, pl.ds(first, count)] = value[done : done + count].astype(jnp.bfloat16)
            done += count


def inner_kernel(members, x_ref, prev_ref, pair_ref, lines_ref, params_ref, weight_ref, hidden_ref, act_ref, mixed_ref):
    rows = x_ref.shape[1]
    leading, _, _ = at_ends()
    pair_at, _, _, _ = places(rows)
    norm = scaling(lines_ref, params_ref, 0, members)

    def row(at, before, own):
        before = [jnp.where(leading, own[0], x) for x in before]
        mixed_frames(act_ref, at, [activated(x, *norm) for x in before + own])

    for r in range(rows):
        row(r + 2, [prev_ref[f, r] for f in range(2)], [x_ref[f, r] for f in range(2)])
    for r in range(2):
        row(pair_at + r, [pair_ref[f, r] for f in (0, 1)], [pair_ref[f, r] for f in (2, 3)])
    mix_weight(weight_ref, mixed_ref)
    first_rows(act_ref, hidden_ref, weight_ref, mixed_ref, [(2, rows - 2), (jnp.minimum(pair_at, rows), 2)])


def outer_kernel(members, x_ref, prev_ref, cross_ref, lines_ref, params_ref, weight_ref, mixed_ref, _, __,
                 hidden_ref, act_ref, line_ref):
    frames, rows, _, channels = x_ref.shape
    leading, top, bottom = at_ends()
    _, cross_at, _, _ = places(rows)
    norm = scaling(lines_ref, params_ref, 0, members)
    for r in range(2):
        rim = [jnp.where(top, ref[f, 0], ref[f, rows - 1]) for ref in (prev_ref, x_ref) for f in range(2)]
        values = [jnp.where(top | bottom, rim[f], cross_ref[f, r]) for f in range(4)]
        before = [jnp.where(leading, values[2], x) for x in values[:2]]
        mixed_frames(act_ref, cross_at + r, [activated(x, *norm) for x in before + values[2:]])
    first_rows(act_ref, hidden_ref, weight_ref, mixed_ref, [(jnp.minimum(cross_at, rows), 2)])
    reads = [functools.partial(lambda f, r: hidden_ref[f, r + 1], f, r) for f in range(frames) for r in range(rows)]
    line_ref[...] = jnp.broadcast_to(local_moments(reads, channels), line_ref.shape)


def second_kernel(members, hidden_ref, prev_ref, lines_ref, params_ref, x_ref, weight_ref, out_ref,
                  act_ref, mixed_ref, made_ref, out_sems):
    frames, rows, cols, channels = x_ref.shape
    leading, top, bottom = at_ends()
    norm = scaling(lines_ref, params_ref, 1, members)

    def row_of(f, r):
        ref = prev_ref if f < 2 else hidden_ref
        if r == 0:
            return jnp.where(top, ref[f % 2, 1], ref[f % 2, 0])
        if r == rows + 1:
            return jnp.where(bottom, ref[f % 2, rows], ref[f % 2, rows + 1])
        return ref[f % 2, r]

    for r in range(rows + 2):
        own = [row_of(f, r) for f in (2, 3)]
        before = [jnp.where(leading, own[0], row_of(f, r)) for f in (0, 1)]
        mixed_frames(act_ref, r, [activated(x, *norm) for x in before + own])
    mix_weight(weight_ref, mixed_ref)
    outs = []
    for f, value in enumerate(convolved(act_ref, weight_ref, mixed_ref, [(0, rows)])):
        made_ref[f] = (x_ref[f].astype(jnp.float32) + value).astype(jnp.bfloat16)
        outs.append(pltpu.make_async_copy(made_ref.at[f], out_ref.at[f], out_sems.at[f]))
        outs[-1].start()
    for copy in outs:
        copy.wait()


def local(
    features, first_gain, first_shift, first_weight, second_gain, second_shift, second_weight
):
    frames, rows, cols, channels = features.shape
    outputs = first_weight.shape[-1]
    tm, band = lax.axis_size("tm"), lax.axis_size("band")
    members = frames * rows * cols * (channels // GROUPS)
    vmem = pl.BlockSpec(memory_space=pltpu.VMEM)
    hbm = pl.BlockSpec(memory_space=pltpu.HBM)
    anywhere = pl.BlockSpec(memory_space=pl.ANY)
    params = pltpu.CompilerParams(vmem_limit_bytes=VMEM_LIMIT)
    small = pltpu.CompilerParams(vmem_limit_bytes=4 * 1024 * 1024)
    line = lambda count: jax.ShapeDtypeStruct((count, LANES), jnp.float32)
    block = lambda f, r: jax.ShapeDtypeStruct((f, r, cols, channels), jnp.bfloat16)
    held = lambda f, r: pltpu.VMEM((f, r, cols, channels), jnp.bfloat16)
    dmas = lambda count: pltpu.SemaphoreType.DMA((count,))
    taps = lambda weight: weight.reshape(9, 3, channels, outputs)
    mixed = pltpu.VMEM((2, 3, 3, channels, outputs), jnp.bfloat16)
    stay = lambda value: pltpu.with_memory_space_constraint(value, pltpu.HBM)
    vectors = [v.reshape(1, channels) for v in (first_gain, first_shift, second_gain, second_shift)]

    lines, kept, vectors = pl.pallas_call(
        stats_kernel,
        out_shape=[line(64), block(frames, rows), jax.ShapeDtypeStruct((8, channels), jnp.float32)],
        in_specs=[hbm] * 5,
        out_specs=[vmem] * 3,
        scratch_shapes=[dmas(frames + 4)],
        compiler_params=small,
        name="moments",
    )(stay(features), *[stay(v) for v in vectors])
    prev = next_frames(kept)
    others = [[(4 * x + y) * band + b for x in range(4) for b in range(band)] for y in range(4)]
    over_others = lambda lines: lax.all_to_all(lines, ("tm", "band"), 0, 0, tiled=True, axis_index_groups=others)
    around = lambda line, by: lax.ppermute(line, "tm", [(i, i - i % 4 + (i + by) % 4) for i in range(tm)])

    def over_y(lines, members, count, *ready):
        return pl.pallas_call(
            functools.partial(ring_merge_kernel, members),
            out_shape=line(count),
            in_specs=[vmem] * (4 + len(ready)),
            out_specs=vmem,
            compiler_params=small,
            cost_estimate=pl.CostEstimate(flops=20 * 10**9, bytes_accessed=0, transcendentals=0),
            name="merge_y",
        )(lines, *[around(lines, by) for by in (2, 1, 3)], *ready)

    lines = pl.pallas_call(
        functools.partial(merge_kernel, members),
        out_shape=line(8),
        in_specs=[vmem],
        out_specs=vmem,
        compiler_params=small,
        name="merge",
    )(over_others(lines))
    cross, pair = pl.pallas_call(
        edges_kernel,
        out_shape=[block(frames + 2, 2), block(frames + 2, 2)],
        in_specs=[vmem] * 3,
        out_specs=[vmem] * 2,
        compiler_params=small,
        cost_estimate=pl.CostEstimate(flops=4 * 10**9, bytes_accessed=0, transcendentals=0),
        name="edges",
    )(kept, prev, lines)
    cross = swapped(cross, "band", 1)
    pair = swapped(pair, "band", 0)
    first_weight = taps(first_weight)
    lines = over_y(lines, 64 * members, 8, first_weight, pair)

    hidden, act, mixed_weight = pl.pallas_call(
        functools.partial(inner_kernel, members),
        out_shape=[
            block(frames, rows + 2),
            block(4, rows + 4),
            jax.ShapeDtypeStruct((2, 3, 3, channels, outputs), jnp.bfloat16),
        ],
        in_specs=[vmem] * 6,
        out_specs=[vmem] * 3,
        compiler_params=params,
        name="first_conv_inner",
    )(kept, prev, pair, lines, vectors, first_weight)
    hidden, _, lines = pl.pallas_call(
        functools.partial(outer_kernel, members),
        out_shape=[block(frames, rows + 2), block(4, rows + 4), line(8)],
        in_specs=[vmem] * 9,
        out_specs=[vmem] * 3,
        input_output_aliases={7: 0, 8: 1},
        compiler_params=params,
        name="first_conv_outer",
    )(kept, prev, cross, lines, vectors, first_weight, mixed_weight, hidden, act)

    prev = next_frames(hidden)
    lines = over_others(over_y(lines, members, 64))

    return pl.pallas_call(
        functools.partial(second_kernel, members),
        out_shape=block(frames, rows),
        in_specs=[vmem] * 6,
        out_specs=hbm,
        scratch_shapes=[held(4, rows + 2), mixed, held(frames, rows), dmas(frames)],
        compiler_params=params,
        name="second_conv",
    )(hidden, prev, lines, vectors, kept, taps(second_weight))


def solution(mesh):
    in_specs = (P("tm", "band", None, None), P(), P(), P(), P(), P(), P())
    out_specs = P("tm", "band", None, None)
    return jax.shard_map(local, mesh=mesh, in_specs=in_specs, out_specs=out_specs, check_vma=False)
```

```python
import functools

import jax
import jax.numpy as jnp
from jax import lax
from jax.experimental import pallas as pl
from jax.experimental.pallas import tpu as pltpu
from jax.sharding import PartitionSpec as P

GROUPS = 32
EPSILON = 1e-06
LANES = 128
VMEM_LIMIT = 32 * 1024 * 1024


def next_frames(value):
    count = lax.axis_size("tm")
    return lax.ppermute(value, "tm", [(i, i + 1) for i in range(count - 1)])


def swapped(value, axis, first):
    count = lax.axis_size(axis)
    pairs = []
    for i in range(first, count - 1, 2):
        pairs += [(i, i + 1), (i + 1, i)]
    return lax.ppermute(value, axis, pairs)


def indicator(rows, cols, fn):
    r = lax.broadcasted_iota(jnp.int32, (rows, cols), 0)
    c = lax.broadcasted_iota(jnp.int32, (rows, cols), 1)
    return jnp.where(fn(r, c), 1.0, 0.0).astype(jnp.bfloat16)


def picked(line, pick):
    parts = []
    for _ in range(3):
        parts.append(line.astype(jnp.bfloat16).astype(jnp.float32))
        line = line - parts[-1]
    row = lax.broadcasted_iota(jnp.int32, (16, line.shape[1]), 0)
    stacked = jnp.where(row == 0, parts[0], jnp.where(row == 1, parts[1], jnp.where(row == 2, parts[2], 0.0)))
    product = jnp.dot(stacked.astype(jnp.bfloat16), pick, preferred_element_type=jnp.float32)
    return jnp.sum(product, axis=0, keepdims=True)


def folded(block):
    cols, channels = block.shape
    return jnp.sum(block.reshape(cols // 8, 8, channels), axis=0)


def channel_sums(rows):
    total = folded(rows[0]().astype(jnp.float32))
    for row in rows[1:]:
        total = total + folded(row().astype(jnp.float32))
    positions = len(rows) * rows[0]().shape[0]
    centre = jnp.sum(total, axis=0, keepdims=True) * (1.0 / positions)
    spread = None
    for row in rows:
        off = row().astype(jnp.float32) - centre
        part = folded(off * off)
        spread = part if spread is None else spread + part
    return centre, jnp.sum(spread, axis=0, keepdims=True), positions


def group_line(centre, spread, positions):
    channels = centre.shape[1]
    size = channels // GROUPS
    same = indicator(channels, channels, lambda r, c: r // size == c // size)
    first = indicator(channels, LANES, lambda r, c: r // size == c)
    second = indicator(channels, LANES, lambda r, c: r // size + GROUPS == c)
    apart = centre - picked(centre, same) * (1.0 / size)
    spread = spread + positions * apart * apart
    return picked(centre, first) * (1.0 / size) + picked(spread, second)


def merged_lines(lines, members):
    count = lines.shape[0]
    total = jnp.sum(lines, axis=0, keepdims=True)
    mean = total * (1.0 / count)
    off = lines - mean
    between = jnp.sum(off * off, axis=0, keepdims=True) * members
    lane = lax.broadcasted_iota(jnp.int32, (1, LANES), 1)
    between = jnp.broadcast_to(between, (8, LANES))
    between = pltpu.roll(between, GROUPS, 1)[:1]
    return jnp.where(lane < GROUPS, mean, jnp.where(lane < 2 * GROUPS, total + between, 0.0))


def channel_moments(line, members, channels):
    size = channels // GROUPS
    pick = indicator(LANES, 2 * channels, lambda r, c: c // size == r)
    wide = picked(line, pick)
    centre, variance = wide[:, :channels], wide[:, channels:] * (1.0 / members)
    return centre, lax.rsqrt(variance + EPSILON)


def activated(x, centre, scale, offset):
    half = (x.astype(jnp.float32) - centre) * scale + offset
    return half + half * jnp.tanh(half)


def mixed_frames(act_ref, row, frames):
    first, second, third, fourth = frames
    for part, value in enumerate((first - third, second + third, third - second, second - fourth)):
        act_ref[part, row] = value.astype(jnp.bfloat16)


def mix_weight(weight_ref, mixed_ref):
    for t in range(9):
        first, middle, last = (weight_ref[3 * i + t // 3, t % 3].astype(jnp.float32) for i in range(3))
        ends = 0.5 * (first + last)
        middle = 0.5 * middle
        mixed_ref[0, t // 3, t % 3] = (ends + middle).astype(jnp.bfloat16)
        mixed_ref[1, t // 3, t % 3] = (ends - middle).astype(jnp.bfloat16)


def convolved(act_ref, weight_ref, mixed_ref, pieces):
    cols, channels = act_ref.shape[2:]
    row_count = sum(count for _, count in pieces)
    windows = [
        jnp.concatenate(
            [
                jnp.concatenate(
                    [act_ref[part, pl.ds(first + j, count)].reshape(count * cols, channels) for first, count in pieces]
                )
                for j in range(3)
            ],
            axis=-1,
        )
        for part in range(4)
    ]
    early = late = None
    for k in range(3):
        taps = weight_ref[0:3, k], mixed_ref[0, :, k], mixed_ref[1, :, k], weight_ref[6:9, k]
        first, second, third, fourth = (
            jnp.dot(window, tap.reshape(3 * channels, -1), preferred_element_type=jnp.float32).reshape(row_count, cols, -1)
            for window, tap in zip(windows, taps)
        )
        pair = first + second + third, second - third - fourth
        if k != 1:
            column = lax.broadcasted_iota(jnp.int32, first.shape, 1)
            edge, by = (0, 1) if k == 0 else (cols - 1, cols - 1)
            pair = [jnp.where(column == edge, value, pltpu.roll(value, by, 1)) for value in pair]
        early = pair[0] if early is None else early + pair[0]
        late = pair[1] if late is None else late + pair[1]
    return early, late


def places(rows):
    even = lax.rem(lax.axis_index("band"), 2) == 0
    pair_at, cross_at = jnp.where(even, rows + 2, 0), jnp.where(even, 0, rows + 2)
    pair_from, cross_from = jnp.where(even, rows - 2, 0), jnp.where(even, 0, rows - 2)
    return pair_at, cross_at, pair_from, cross_from


def stats_kernel(x_ref, *refs):
    vectors, (line_ref, kept_ref, params_ref, sems) = refs[:4], refs[4:]
    frames, rows, _, channels = x_ref.shape
    copies = [pltpu.make_async_copy(x_ref.at[f], kept_ref.at[f], sems.at[f]) for f in range(frames)]
    copies += [
        pltpu.make_async_copy(vector, params_ref.at[pl.ds(i, 1)], sems.at[frames + i])
        for i, vector in enumerate(vectors)
    ]
    for copy in copies:
        copy.start()
    for copy in copies:
        copy.wait()
    reads = [functools.partial(lambda f, r: kept_ref[f, r], f, r) for f in range(frames) for r in range(rows)]
    line_ref[...] = jnp.broadcast_to(group_line(*channel_sums(reads)), line_ref.shape)


def edges_kernel(x_ref, prev_ref, after_ref, cross_ref, pair_ref):
    _, _, pair_from, cross_from = places(x_ref.shape[1])
    for out_ref, at in ((pair_ref, pair_from), (cross_ref, cross_from)):
        out_ref[0:2] = prev_ref[:, pl.ds(at, 2)]
        out_ref[2:4] = x_ref[:, pl.ds(at, 2)]


def ring_merge_kernel(members, a_ref, b_ref, c_ref, d_ref, *refs):
    lines = jnp.concatenate([r[0:1] for r in (a_ref, b_ref, c_ref, d_ref)], axis=0)
    refs[-1][...] = jnp.broadcast_to(merged_lines(lines, members), refs[-1].shape)


def merge_kernel(members, lines_ref, line_ref):
    line_ref[...] = jnp.broadcast_to(merged_lines(lines_ref[...], members), line_ref.shape)


def scaling(lines_ref, params_ref, norm, members):
    channels = params_ref.shape[1]
    devices = lax.axis_size("tm") * lax.axis_size("band")
    line = merged_lines(lines_ref[...], members * devices // lines_ref.shape[0]) if norm else lines_ref[0:1]
    centre, inverse = channel_moments(line, members * devices, channels)
    gain, shift = params_ref[2 * norm : 2 * norm + 1], params_ref[2 * norm + 1 : 2 * norm + 2]
    return centre, 0.5 * inverse * gain, 0.5 * shift


def at_ends():
    band = lax.axis_index("band")
    return lax.axis_index("tm") == 0, band == 0, band == lax.axis_size("band") - 1


def first_rows(act_ref, out_ref, weight_ref, mixed_ref, pieces):
    for f, value in enumerate(convolved(act_ref, weight_ref, mixed_ref, pieces)):
        done = 0
        for first, count in pieces:
            out_ref[f, pl.ds(first, count)] = value[done : done + count].astype(jnp.bfloat16)
            done += count


def inner_kernel(members, x_ref, prev_ref, pair_ref, lines_ref, params_ref, weight_ref, hidden_ref, act_ref, mixed_ref,
                 sums_ref):
    rows = x_ref.shape[1]
    leading, _, _ = at_ends()
    pair_at, _, _, _ = places(rows)
    norm = scaling(lines_ref, params_ref, 0, members)

    def row(at, before, own):
        before = [jnp.where(leading, own[0], x) for x in before]
        mixed_frames(act_ref, at, [activated(x, *norm) for x in before + own])

    for r in range(rows):
        row(r + 2, [prev_ref[f, r] for f in range(2)], [x_ref[f, r] for f in range(2)])
    for r in range(2):
        row(pair_at + r, [pair_ref[f, r] for f in (0, 1)], [pair_ref[f, r] for f in (2, 3)])
    mix_weight(weight_ref, mixed_ref)
    first_rows(act_ref, hidden_ref, weight_ref, mixed_ref, [(2, rows - 2), (jnp.minimum(pair_at, rows), 2)])
    near = jnp.where(pair_at == 0, 1, rows)
    places_own = [(f, r) for f in range(2) for r in list(range(2, rows)) + [near]]
    centre, spread, _ = channel_sums([functools.partial(lambda f, r: hidden_ref[f, r], *at) for at in places_own])
    for i, value in enumerate((centre, spread) + norm):
        sums_ref[i : i + 1] = value


def outer_kernel(x_ref, prev_ref, cross_ref, sums_ref, weight_ref, mixed_ref, _, __, hidden_ref, act_ref, line_ref):
    frames, rows, cols, _ = x_ref.shape
    leading, top, bottom = at_ends()
    _, cross_at, _, _ = places(rows)
    first_centre, first_spread, *norm = [sums_ref[i : i + 1] for i in range(5)]
    for r in range(2):
        rim = [jnp.where(top, ref[f, 0], ref[f, rows - 1]) for ref in (prev_ref, x_ref) for f in range(2)]
        values = [jnp.where(top | bottom, rim[f], cross_ref[f, r]) for f in range(4)]
        before = [jnp.where(leading, values[2], x) for x in values[:2]]
        mixed_frames(act_ref, cross_at + r, [activated(x, *norm) for x in before + values[2:]])
    first_rows(act_ref, hidden_ref, weight_ref, mixed_ref, [(jnp.minimum(cross_at, rows), 2)])
    near = jnp.where(cross_at == 0, 1, rows)
    centre, spread, count = channel_sums([functools.partial(lambda f: hidden_ref[f, near], f) for f in range(frames)])
    positions = frames * rows * cols
    apart = centre - first_centre
    share = count / positions
    spread = first_spread + spread + (positions - count) * share * apart * apart
    line_ref[...] = jnp.broadcast_to(group_line(first_centre + share * apart, spread, positions), line_ref.shape)


def second_kernel(members, hidden_ref, prev_ref, lines_ref, params_ref, x_ref, weight_ref, out_ref,
                  act_ref, mixed_ref, made_ref, out_sems):
    frames, rows, cols, channels = x_ref.shape
    leading, top, bottom = at_ends()
    norm = scaling(lines_ref, params_ref, 1, members)

    def row_of(f, r):
        ref = prev_ref if f < 2 else hidden_ref
        if r == 0:
            return jnp.where(top, ref[f % 2, 1], ref[f % 2, 0])
        if r == rows + 1:
            return jnp.where(bottom, ref[f % 2, rows], ref[f % 2, rows + 1])
        return ref[f % 2, r]

    for r in range(rows + 2):
        own = [row_of(f, r) for f in (2, 3)]
        before = [jnp.where(leading, own[0], row_of(f, r)) for f in (0, 1)]
        mixed_frames(act_ref, r, [activated(x, *norm) for x in before + own])
    mix_weight(weight_ref, mixed_ref)
    outs = []
    for f, value in enumerate(convolved(act_ref, weight_ref, mixed_ref, [(0, rows)])):
        made_ref[f] = (x_ref[f].astype(jnp.float32) + value).astype(jnp.bfloat16)
        outs.append(pltpu.make_async_copy(made_ref.at[f], out_ref.at[f], out_sems.at[f]))
        outs[-1].start()
    for copy in outs:
        copy.wait()


def local(
    features, first_gain, first_shift, first_weight, second_gain, second_shift, second_weight
):
    frames, rows, cols, channels = features.shape
    outputs = first_weight.shape[-1]
    tm, band = lax.axis_size("tm"), lax.axis_size("band")
    members = frames * rows * cols * (channels // GROUPS)
    vmem = pl.BlockSpec(memory_space=pltpu.VMEM)
    hbm = pl.BlockSpec(memory_space=pltpu.HBM)
    anywhere = pl.BlockSpec(memory_space=pl.ANY)
    params = pltpu.CompilerParams(vmem_limit_bytes=VMEM_LIMIT)
    small = pltpu.CompilerParams(vmem_limit_bytes=4 * 1024 * 1024)
    line = lambda count: jax.ShapeDtypeStruct((count, LANES), jnp.float32)
    block = lambda f, r: jax.ShapeDtypeStruct((f, r, cols, channels), jnp.bfloat16)
    held = lambda f, r: pltpu.VMEM((f, r, cols, channels), jnp.bfloat16)
    dmas = lambda count: pltpu.SemaphoreType.DMA((count,))
    taps = lambda weight: weight.reshape(9, 3, channels, outputs)
    mixed = pltpu.VMEM((2, 3, 3, channels, outputs), jnp.bfloat16)
    stay = lambda value: pltpu.with_memory_space_constraint(value, pltpu.HBM)
    vectors = [v.reshape(1, channels) for v in (first_gain, first_shift, second_gain, second_shift)]

    prev = next_frames(features)
    lines, kept, vectors = pl.pallas_call(
        stats_kernel,
        out_shape=[line(64), block(frames, rows), jax.ShapeDtypeStruct((8, channels), jnp.float32)],
        in_specs=[hbm] * 5,
        out_specs=[vmem] * 3,
        scratch_shapes=[dmas(frames + 4)],
        compiler_params=small,
        name="moments",
    )(stay(features), *[stay(v) for v in vectors])
    others = [[(4 * x + y) * band + b for x in range(4) for b in range(band)] for y in range(4)]
    over_others = lambda lines: lax.all_to_all(lines, ("tm", "band"), 0, 0, tiled=True, axis_index_groups=others)
    around = lambda line, by: lax.ppermute(line, "tm", [(i, i - i % 4 + (i + by) % 4) for i in range(tm)])

    def over_y(lines, members, count, *ready):
        return pl.pallas_call(
            functools.partial(ring_merge_kernel, members),
            out_shape=line(count),
            in_specs=[vmem] * (4 + len(ready)),
            out_specs=vmem,
            compiler_params=small,
            cost_estimate=pl.CostEstimate(flops=20 * 10**9, bytes_accessed=0, transcendentals=0),
            name="merge_y",
        )(lines, *[around(lines, by) for by in (2, 1, 3)], *ready)

    lines = pl.pallas_call(
        functools.partial(merge_kernel, members),
        out_shape=line(8),
        in_specs=[vmem],
        out_specs=vmem,
        compiler_params=small,
        name="merge",
    )(over_others(lines))
    cross, pair = pl.pallas_call(
        edges_kernel,
        out_shape=[block(frames + 2, 2), block(frames + 2, 2)],
        in_specs=[vmem] * 3,
        out_specs=[vmem] * 2,
        compiler_params=small,
        cost_estimate=pl.CostEstimate(flops=4 * 10**9, bytes_accessed=0, transcendentals=0),
        name="edges",
    )(kept, prev, lines)
    cross = swapped(cross, "band", 1)
    pair = swapped(pair, "band", 0)
    first_weight = taps(first_weight)
    lines = over_y(lines, 64 * members, 8, first_weight, pair)

    hidden, act, mixed_weight, sums = pl.pallas_call(
        functools.partial(inner_kernel, members),
        out_shape=[
            block(frames, rows + 2),
            block(4, rows + 4),
            jax.ShapeDtypeStruct((2, 3, 3, channels, outputs), jnp.bfloat16),
            jax.ShapeDtypeStruct((8, channels), jnp.float32),
        ],
        in_specs=[vmem] * 6,
        out_specs=[vmem] * 4,
        compiler_params=params,
        name="first_conv_inner",
    )(kept, prev, pair, lines, vectors, first_weight)
    hidden, _, lines = pl.pallas_call(
        outer_kernel,
        out_shape=[block(frames, rows + 2), block(4, rows + 4), line(8)],
        in_specs=[vmem] * 8,
        out_specs=[vmem] * 3,
        input_output_aliases={6: 0, 7: 1},
        compiler_params=params,
        name="first_conv_outer",
    )(kept, prev, cross, sums, first_weight, mixed_weight, hidden, act)

    prev = next_frames(hidden)
    lines = over_others(over_y(lines, members, 64))

    return pl.pallas_call(
        functools.partial(second_kernel, members),
        out_shape=block(frames, rows),
        in_specs=[vmem] * 6,
        out_specs=hbm,
        scratch_shapes=[held(4, rows + 2), mixed, held(frames, rows), dmas(frames)],
        compiler_params=params,
        name="second_conv",
    )(hidden, prev, lines, vectors, kept, taps(second_weight))


def solution(mesh):
    in_specs = (P("tm", "band", None, None), P(), P(), P(), P(), P(), P())
    out_specs = P("tm", "band", None, None)
    return jax.shard_map(local, mesh=mesh, in_specs=in_specs, out_specs=out_specs, check_vma=False)
```
